256 devices in a mesh: replica: 2 (over z_hi), tpa: 16 (over x, z_lo), tpb: 8 (over y, core).
Axes of the slice: x: 4, y: 4, z: 8 (z_hi: 2, z_lo: 4; z = z_hi * 4 + z_lo), core: 2. Of those that a mesh axis runs over, the one named last changes fastest.
Arguments:
- layer_input: bfloat16 [1024, 8192], P(('replica', 'tpa'), 'tpb'), may hold values from -6 to 6
- gate_weight: bfloat16 [2, 8192, 14336], P('replica', 'tpb', 'tpa'), may hold values from -0.0625 to 0.0625
- up_weight: bfloat16 [2, 8192, 14336], P('replica', 'tpb', 'tpa'), may hold values from -0.0625 to 0.0625
- down_weight: bfloat16 [2, 14336, 8192], P('replica', 'tpa', 'tpb'), may hold values from -0.046875 to 0.046875
- out_grad: bfloat16 [1024, 8192], P(('replica', 'tpa'), 'tpb'), may hold values from -6 to 6
- inner_params: bfloat16 [2, 2, 512, 8192], P('replica', None, 'tpa', 'tpb'), may hold values from -6 to 6
- outer_base: float32 [2, 512, 8192], P(None, 'tpa', 'tpb'), may hold values from -6 to 6
- outer_momentum: float32 [2, 512, 8192], P(None, 'tpa', 'tpb'), may hold values from -4 to 4
- span_index: int32 [1], replicated, may hold values from 0 to 1
Outputs:
- layer_out: bfloat16 [1024, 8192], P(('replica', 'tpa'), 'tpb')
- grad_input: bfloat16 [1024, 8192], P(('replica', 'tpa'), 'tpb')
- grad_gate: bfloat16 [2, 8192, 14336], P('replica', 'tpb', 'tpa')
- grad_up: bfloat16 [2, 8192, 14336], P('replica', 'tpb', 'tpa')
- grad_down: bfloat16 [2, 14336, 8192], P('replica', 'tpa', 'tpb')
- new_base: float32 [512, 8192], P('tpa', 'tpb')
- new_momentum: float32 [512, 8192], P('tpa', 'tpb')
The draws below stay inside these ranges and needn't reach their ends.
Inputs may be any that keep to these rules, and one draw needn't show every extreme that they name: `span_index`: selects one span of the fragment tables.
All inputs are finite; a program needn't handle non-finite values. Where the reference program divides by a largest or mean magnitude, that divisor is 1e-20 or more.
Results may differ from the reference program's by a relative error of at most 0.034.
Values may be sent and summed in bfloat16 or wider, within the bound.
No kernel may reach another device: no remote copies, remote signals or barrier semaphores. Data moves between devices by JAX's collectives and lax.ppermute only.
A program may use at most 64 MiB of HBM per device.

```python
import jax
import jax.numpy as jnp
from jax import lax

D = 8192
FF = 14336
ROWS = 512
FROWS = 512
SPANS = 2
GROUP = 128
TOKENS = 1024
N_REPLICA = 2
N_TPA = 16
N_TPB = 8


def levels(own_key, extent, shards, low, largest):
    factor_of, own = 1.0, jax.random.fold_in(own_key, 6)
    for position, blocks in shards:
        draws = jnp.exp(jax.random.uniform(jax.random.fold_in(own, position), (blocks,), jnp.float32, low / len(shards), largest / len(shards)))
        factor_of = factor_of * jnp.repeat(draws, extent[position] // blocks).reshape([-1 if axis == position else 1 for axis in range(len(extent))])
    return factor_of


def bell_draw(own_key, dims, width, reach, split=(), kind=jnp.bfloat16):
    entries = width * jax.random.normal(own_key, dims, jnp.float32)
    if split:
        entries = entries * levels(own_key, dims, split, -0.22, 0.18)
    return jnp.clip(entries, -reach, reach).astype(kind)


def setup_inputs(seed: int = 0) -> dict:
    keys = jax.random.split(jax.random.key(seed), 10)
    layer_input = bell_draw(keys[0], (TOKENS, D), 1.0, 6.0, ((0, 32), (1, 8)))
    gate_weight = bell_draw(keys[1], (N_REPLICA, D, FF), D ** -0.5, 0.0625, ((0, 2), (1, 8), (2, 16)))
    up_weight = bell_draw(keys[2], (N_REPLICA, D, FF), D ** -0.5, 0.0625, ((0, 2), (1, 8), (2, 16)))
    down_weight = bell_draw(keys[3], (N_REPLICA, FF, D), FF ** -0.5, 0.046875, ((0, 2), (1, 16), (2, 8)))
    out_grad = bell_draw(keys[4], (TOKENS, D), 1.0, 6.0, ((0, 32), (1, 8)))
    inner_params = bell_draw(keys[5], (N_REPLICA, SPANS, FROWS, D), 1.0, 6.0, ((0, 2), (2, 16), (3, 8)))
    outer_base = bell_draw(keys[6], (SPANS, FROWS, D), 1.0, 6.0, ((1, 16), (2, 8)), jnp.float32)
    outer_momentum = bell_draw(keys[7], (SPANS, FROWS, D), 0.5, 4.0, ((1, 16), (2, 8)), jnp.float32)
    span_index = jax.random.randint(keys[8], (1,), 0, SPANS).astype(jnp.int32)
    return dict(layer_input=layer_input, gate_weight=gate_weight, up_weight=up_weight, down_weight=down_weight, out_grad=out_grad, inner_params=inner_params, outer_base=outer_base, outer_momentum=outer_momentum, span_index=span_index)


outer_rate = 0.7
outer_decay = 0.9


def rounded(value):
    return lax.optimization_barrier(value.astype(jnp.bfloat16)).astype(jnp.float32)


def split_sum(pairs, parts):
    row_total = pairs[0][0].shape[0]
    col_total = pairs[0][1].shape[1]
    block_width = pairs[0][0].shape[1] // parts

    def add_block(summed, block_index):
        partial_value = jnp.zeros((row_total, col_total), jnp.float32)
        for left_side, right_side in pairs:
            left_block = lax.dynamic_slice_in_dim(left_side, block_index * block_width, block_width, 1)
            right_block = lax.dynamic_slice_in_dim(right_side, block_index * block_width, block_width, 0)
            partial_value = partial_value + jnp.dot(left_block, right_block, preferred_element_type=jnp.float32)
        return summed + rounded(partial_value), None

    summed, unused = lax.scan(add_block, jnp.zeros((row_total, col_total), jnp.float32), jnp.arange(parts, dtype=jnp.int32))
    return summed


def reference(layer_input, gate_weight, up_weight, down_weight, out_grad, inner_params, outer_base, outer_momentum, span_index):
    out_list, input_list, gate_list, up_list, down_list = [], [], [], [], []
    for replica in range(N_REPLICA):
        rows_in = layer_input[replica * ROWS:(replica + 1) * ROWS]
        grad_rows = out_grad[replica * ROWS:(replica + 1) * ROWS]
        w_gate = gate_weight[replica]
        w_up = up_weight[replica]
        w_down = down_weight[replica]
        gate_sum = split_sum([(rows_in, w_gate)], N_TPB)
        up_sum = split_sum([(rows_in, w_up)], N_TPB)
        sigmoid_gate = jax.nn.sigmoid(gate_sum)
        activated = gate_sum * sigmoid_gate
        hidden_full = (activated * up_sum).astype(jnp.bfloat16)
        down_sum = split_sum([(hidden_full, w_down)], N_TPA)
        out_list.append((rows_in.astype(jnp.float32) + down_sum).astype(jnp.bfloat16))
        hidden_grad = split_sum([(grad_rows, w_down.T)], N_TPB)
        silu_slope = sigmoid_gate * (1.0 + gate_sum * (1.0 - sigmoid_gate))
        grad_gate_h = (hidden_grad * up_sum * silu_slope).astype(jnp.bfloat16)
        grad_up_h = (hidden_grad * activated).astype(jnp.bfloat16)
        gate_list.append(jnp.dot(rows_in.T, grad_gate_h, preferred_element_type=jnp.float32).astype(jnp.bfloat16))
        up_list.append(jnp.dot(rows_in.T, grad_up_h, preferred_element_type=jnp.float32).astype(jnp.bfloat16))
        down_list.append(jnp.dot(hidden_full.T, grad_rows, preferred_element_type=jnp.float32).astype(jnp.bfloat16))
        back_sum = split_sum([(grad_gate_h, w_gate.T), (grad_up_h, w_up.T)], N_TPA)
        input_list.append((grad_rows.astype(jnp.float32) + back_sum).astype(jnp.bfloat16))
    span = span_index[0]
    base_span = lax.dynamic_index_in_dim(outer_base, span, 0, keepdims=False)
    momentum_span = lax.dynamic_index_in_dim(outer_momentum, span, 0, keepdims=False)
    summed_delta = jnp.zeros((FROWS, D // GROUP, GROUP), jnp.float32)
    for replica in range(N_REPLICA):
        inner_span = lax.dynamic_index_in_dim(inner_params[replica], span, 0, keepdims=False).astype(jnp.float32)
        pseudo_delta = (base_span - inner_span).reshape(FROWS, D // GROUP, GROUP)
        block_scale = (jnp.max(jnp.abs(pseudo_delta), axis=2) + 1e-6).astype(jnp.bfloat16)
        code_values = (pseudo_delta / block_scale.astype(jnp.float32)[:, :, None]).astype(jnp.bfloat16)
        summed_delta = summed_delta + code_values.astype(jnp.float32) * block_scale.astype(jnp.float32)[:, :, None]
    mean_delta = summed_delta.reshape(FROWS, D) / N_REPLICA
    new_momentum = outer_decay * momentum_span + mean_delta
    new_base = base_span - outer_rate * (mean_delta + outer_decay * new_momentum)
    return (jnp.concatenate(out_list, 0), jnp.concatenate(input_list, 0), jnp.stack(gate_list), jnp.stack(up_list), jnp.stack(down_list), new_base, new_momentum)
```

```python
import jax
import jax.numpy as jnp
from jax import lax
from jax.sharding import PartitionSpec as P

GROUP = 128
outer_rate = 0.7
outer_decay = 0.9
F32 = jnp.float32
BF16 = jnp.bfloat16


def shift_x(values, step):
    return lax.ppermute(values, "tpa", [(i, (i // 4 + step) % 4 * 4 + i % 4) for i in range(16)])


def shift_z(values, step):
    return lax.ppermute(values, "tpa", [(i, i // 4 * 4 + (i + step) % 4) for i in range(16)])


def shift_y(values, step):
    return lax.ppermute(values, "tpb", [(i, (i // 2 + step) % 4 * 2 + i % 2) for i in range(8)])


def swap_core(values):
    return lax.ppermute(values, "tpb", [(i, i ^ 1) for i in range(8)])


def ring_gather(own, shift):
    half = own.shape[0] // 2
    above = shift(own, -1)
    below = shift(own, 1)
    far_top = shift(above[:half], -1)
    far_bottom = shift(below[half:], 1)
    return own, above, below, far_top, far_bottom


def ring_scatter(far, above, below, own, shift):
    half = far.shape[0] // 2
    from_below = shift(far[:half].astype(BF16), 1).astype(F32)
    from_above = shift(far[half:].astype(BF16), -1).astype(F32)
    above = jnp.concatenate([above[:half] + from_below, above[half:]], axis=0)
    below = jnp.concatenate([below[:half], below[half:] + from_above], axis=0)
    got_below = shift(above.astype(BF16), 1)
    got_above = shift(below.astype(BF16), -1)
    return own + got_below.astype(F32) + got_above.astype(F32)


def gather_tokens(values):
    near = jnp.concatenate([values] + [shift_z(values, -dz) for dz in (1, 2, 3)], axis=0)
    return jnp.concatenate(ring_gather(near, shift_x), axis=0)


def scatter_tokens(lhs_rhs):
    def rows(start, stop):
        total = None
        for lhs, rhs, dims in lhs_rhs:
            term = lax.dot_general(lhs[start:stop], rhs, dims, preferred_element_type=F32)
            total = term if total is None else total + term
        return total

    far = rows(384, 512)
    sides = rows(128, 384)
    own = rows(0, 128)
    line = ring_scatter(far, sides[:128], sides[128:], own, shift_x)
    total = line[:32]
    for dz in (1, 2, 3):
        total = total + shift_z(line[dz * 32 : (dz + 1) * 32].astype(BF16), dz).astype(F32)
    return total


def core_sum(lhs, rhs, dims, core):
    other = lax.dynamic_slice_in_dim(lhs, (1 - core) * 256, 256, 0)
    mine = lax.dynamic_slice_in_dim(lhs, core * 256, 256, 0)
    sent = lax.dot_general(other, rhs, dims, preferred_element_type=F32).astype(BF16)
    got = swap_core(sent)
    return lax.dot_general(mine, rhs, dims, preferred_element_type=F32) + got.astype(F32)


def scatter_hidden(parts, place):
    stacked = [part.reshape(4, 64, part.shape[1]) for part in parts]

    def block(offset):
        picks = [
            lax.dynamic_index_in_dim(part, lax.rem(place + offset, 4), 0, keepdims=False)
            for part in stacked
        ]
        return jnp.concatenate([p[:32] for p in picks] + [p[32:] for p in picks], axis=0)

    total = ring_scatter(block(2), block(1), block(3), block(0), shift_y)
    count = len(parts)
    return [
        jnp.concatenate([total[32 * i : 32 * (i + 1)], total[32 * (count + i) : 32 * (count + i + 1)]], axis=0)
        for i in range(count)
    ]


def gather_hidden(values, place, core):
    count, _, width = values.shape
    flat = values.reshape(count * 64, width)
    own, above, below, far_top, far_bottom = ring_gather(flat, shift_y)
    far = jnp.concatenate([far_top, far_bottom], axis=0)
    ring = jnp.stack([own, above, far, below]).reshape(4, count, 64, width)
    turned = lax.dynamic_slice_in_dim(jnp.concatenate([ring, ring], axis=0), lax.rem(4 - place, 4), 4, 0)
    mine = turned.transpose(1, 0, 2, 3).reshape(count, 256, width)
    other = swap_core(mine)
    low = jnp.where(core == 0, mine, other)
    high = jnp.where(core == 0, other, mine)
    return jnp.concatenate([low, high], axis=1)


def body(
    layer_input,
    gate_weight,
    up_weight,
    down_weight,
    out_grad,
    inner_params,
    outer_base,
    outer_momentum,
    span_index,
):
    w_gate = gate_weight[0]
    w_up = up_weight[0]
    w_down = down_weight[0]
    place = lax.axis_index("tpb") // 2
    core = lax.axis_index("tpb") % 2
    plain = (((1,), (0,)), ((), ()))
    turned = (((1,), (1,)), ((), ()))

    rows_in = gather_tokens(layer_input)
    grad_rows = gather_tokens(out_grad)

    gate_half = core_sum(rows_in, w_gate, plain, core)
    up_half = core_sum(rows_in, w_up, plain, core)
    gate_sum, up_sum = scatter_hidden([gate_half, up_half], place)
    back_half = core_sum(grad_rows, w_down, turned, core)
    (hidden_grad,) = scatter_hidden([back_half], place)

    sigmoid_gate = jax.nn.sigmoid(gate_sum)
    activated = gate_sum * sigmoid_gate
    hidden_part = (activated * up_sum).astype(BF16)
    hidden_full = gather_hidden(hidden_part[None], place, core)[0]
    silu_slope = sigmoid_gate * (1.0 + gate_sum * (1.0 - sigmoid_gate))
    grad_part = jnp.stack(
        [(hidden_grad * up_sum * silu_slope).astype(BF16), (hidden_grad * activated).astype(BF16)]
    )
    grad_hidden = gather_hidden(grad_part, place, core)
    grad_gate_h = grad_hidden[0]
    grad_up_h = grad_hidden[1]

    layer_out = (layer_input.astype(F32) + scatter_tokens([(hidden_full, w_down, plain)])).astype(BF16)
    grad_input = (
        out_grad.astype(F32)
        + scatter_tokens([(grad_gate_h, w_gate, turned), (grad_up_h, w_up, turned)])
    ).astype(BF16)

    rows_turned = lax.optimization_barrier(rows_in.T)
    grad_gate = jnp.dot(rows_turned, grad_gate_h, preferred_element_type=F32).astype(BF16)[None]
    grad_up = jnp.dot(rows_turned, grad_up_h, preferred_element_type=F32).astype(BF16)[None]
    grad_down = lax.dot_general(
        hidden_full, grad_rows, (((0,), (0,)), ((), ())), preferred_element_type=F32
    ).astype(BF16)[None]

    span = span_index[0]
    inner_span = lax.dynamic_index_in_dim(inner_params[0], span, 0, keepdims=False).astype(F32)
    base_span = lax.dynamic_index_in_dim(outer_base, span, 0, keepdims=False)
    momentum_span = lax.dynamic_index_in_dim(outer_momentum, span, 0, keepdims=False)
    frag_rows, frag_cols = base_span.shape
    pseudo_delta = (base_span - inner_span).reshape(frag_rows, frag_cols // GROUP, GROUP)
    block_scale = (jnp.max(jnp.abs(pseudo_delta), axis=2) + 1e-06).astype(BF16)
    wide_scale = block_scale.astype(F32)[:, :, None]
    code_values = (pseudo_delta / wide_scale).astype(BF16)
    decoded = (code_values.astype(F32) * wide_scale).astype(BF16).reshape(frag_rows, frag_cols)
    other = lax.ppermute(decoded, "replica", [(0, 1), (1, 0)])
    mean_delta = (decoded.astype(F32) + other.astype(F32)) / 2
    new_momentum = outer_decay * momentum_span + mean_delta
    new_base = base_span - outer_rate * (mean_delta + outer_decay * new_momentum)
    return (layer_out, grad_input, grad_gate, grad_up, grad_down, new_base, new_momentum)


def solution(mesh):
    return jax.shard_map(
        body,
        mesh=mesh,
        in_specs=(
            P(("replica", "tpa"), "tpb"),
            P("replica", "tpb", "tpa"),
            P("replica", "tpb", "tpa"),
            P("replica", "tpa", "tpb"),
            P(("replica", "tpa"), "tpb"),
            P("replica", None, "tpa", "tpb"),
            P(None, "tpa", "tpb"),
            P(None, "tpa", "tpb"),
            P(),
        ),
        out_specs=(
            P(("replica", "tpa"), "tpb"),
            P(("replica", "tpa"), "tpb"),
            P("replica", "tpb", "tpa"),
            P("replica", "tpb", "tpa"),
            P("replica", "tpa", "tpb"),
            P("tpa", "tpb"),
            P("tpa", "tpb"),
        ),
        check_vma=False,
    )
```

```python
import jax
import jax.numpy as jnp
from jax import lax
from jax.sharding import PartitionSpec as P

GROUP = 128
outer_rate = 0.7
outer_decay = 0.9
F32 = jnp.float32
BF16 = jnp.bfloat16


def shift_x(values, step):
    return lax.ppermute(values, "tpa", [(i, (i // 4 + step) % 4 * 4 + i % 4) for i in range(16)])


def shift_z(values, step):
    return lax.ppermute(values, "tpa", [(i, i // 4 * 4 + (i + step) % 4) for i in range(16)])


def shift_y(values, step):
    return lax.ppermute(values, "tpb", [(i, (i // 2 + step) % 4 * 2 + i % 2) for i in range(8)])


def shift_sides(values):
    return lax.ppermute(values, "tpb", [(i, (i // 2 + 1 + 2 * (i % 2)) % 4 * 2 + i % 2) for i in range(8)])


def swap_core(values):
    return lax.ppermute(values, "tpb", [(i, i ^ 1) for i in range(8)])


def after(values, *earlier):
    return lax.optimization_barrier((values,) + earlier)[0]


def gather_near(values):
    return jnp.concatenate([values] + [shift_z(values, -dz) for dz in (1, 2, 3)], axis=0)


def gather_far(near):
    return jnp.concatenate([near, shift_x(near, -1), shift_x(near, 1), shift_x(near, 2)], axis=0)


def block(rows, index):
    return lax.dynamic_slice_in_dim(rows, lax.rem(index, 4) * 128, 128, 0)


def half_block(rows, index, core):
    return lax.dynamic_slice_in_dim(rows, lax.rem(index, 4) * 128 + core * 64, 64, 0)


def scatter_hidden(partial, place, core):
    near = place + 1 + 2 * core
    sent = jnp.concatenate(
        [
            block(partial, near + 2),
            half_block(partial, place + 2, 1 - core),
            half_block(partial, place, 1 - core),
        ],
        axis=0,
    ).astype(BF16)
    got = swap_core(sent).astype(F32)
    across = shift_y((half_block(partial, place + 2, core) + got[128:192]).astype(BF16), 2)
    beside = shift_sides((block(partial, near) + got[:128]).astype(BF16))
    mine = half_block(partial, place, core) + got[192:]
    kept = lax.dynamic_slice_in_dim(beside, core * 64, 64, 0)
    given = lax.dynamic_slice_in_dim(beside, (1 - core) * 64, 64, 0)
    return mine + across.astype(F32) + kept.astype(F32) + swap_core(given).astype(F32)


def gather_hidden(own, place, core):
    across = shift_y(own, 2)
    sibling = swap_core(own)
    first = core == 0
    pair = jnp.concatenate([jnp.where(first, own, sibling), jnp.where(first, sibling, own)], axis=0)
    beside = shift_sides(pair)
    swapped = swap_core(jnp.concatenate([beside, across], axis=0))
    far = swapped[128:]
    ring = [
        pair,
        jnp.where(first, swapped[:128], beside),
        jnp.where(first, across, far),
        jnp.where(first, far, across),
        jnp.where(first, beside, swapped[:128]),
    ]
    rows = jnp.concatenate(ring, axis=0)
    return lax.dynamic_slice_in_dim(jnp.concatenate([rows, rows], axis=0), lax.rem(4 - place, 4) * 128, 512, 0)


def scatter_far(rows, weight, dims):
    def part(index):
        return lax.dot_general(rows[index * 128 : (index + 1) * 128], weight, dims, preferred_element_type=F32)

    return [part(3).astype(BF16), part(1).astype(BF16), part(2).astype(BF16)], part(0)


def add_far(sent, own):
    return (
        own
        + shift_x(sent[0], 2).astype(F32)
        + shift_x(sent[1], 1).astype(F32)
        + shift_x(sent[2], -1).astype(F32)
    )


def scatter_near(line):
    total = line[:32]
    for dz in (1, 2, 3):
        total = total + shift_z(line[dz * 32 : (dz + 1) * 32].astype(BF16), dz).astype(F32)
    return total


def body(
    layer_input,
    gate_weight,
    up_weight,
    down_weight,
    out_grad,
    inner_params,
    outer_base,
    outer_momentum,
    span_index,
):
    w_both = jnp.concatenate([gate_weight[0], up_weight[0]], axis=1)
    w_down = down_weight[0]
    width = w_down.shape[0]
    place = lax.axis_index("tpb") // 2
    core = lax.axis_index("tpb") % 2
    plain = (((1,), (0,)), ((), ()))
    turned = (((1,), (1,)), ((), ()))

    near_in = gather_near(layer_input)
    near_grad = gather_near(after(out_grad, near_in))
    rows_in = gather_far(near_in)
    grad_rows = gather_far(near_grad)

    projected = jnp.dot(rows_in, w_both, preferred_element_type=F32)
    projected = scatter_hidden(projected, place, core)
    gate_sum = projected[:, :width]
    up_sum = projected[:, width:]
    hidden_grad = lax.dot_general(grad_rows, w_down, turned, preferred_element_type=F32)
    hidden_grad = scatter_hidden(hidden_grad, place, core)

    sigmoid_gate = jax.nn.sigmoid(gate_sum)
    activated = gate_sum * sigmoid_gate
    hidden_part = (activated * up_sum).astype(BF16)
    hidden_full = gather_hidden(hidden_part, place, core)
    silu_slope = sigmoid_gate * (1.0 + gate_sum * (1.0 - sigmoid_gate))
    grad_part = jnp.concatenate(
        [(hidden_grad * up_sum * silu_slope).astype(BF16), (hidden_grad * activated).astype(BF16)], axis=1
    )
    grad_hidden = gather_hidden(grad_part, place, core)

    out_sent, out_own = scatter_far(hidden_full, w_down, plain)
    in_sent, in_own = scatter_far(grad_hidden, w_both, turned)
    out_line = add_far(out_sent, out_own)
    in_line = add_far(in_sent, in_own)
    layer_out = (layer_input.astype(F32) + scatter_near(after(out_line, *in_sent))).astype(BF16)
    grad_input = (out_grad.astype(F32) + scatter_near(in_line)).astype(BF16)

    rows_turned = lax.optimization_barrier(rows_in.T)
    grad_gate = jnp.dot(rows_turned, grad_hidden[:, :width], preferred_element_type=F32).astype(BF16)[None]
    grad_up = jnp.dot(rows_turned, grad_hidden[:, width:], preferred_element_type=F32).astype(BF16)[None]
    grad_down = lax.dot_general(
        hidden_full, grad_rows, (((0,), (0,)), ((), ())), preferred_element_type=F32
    ).astype(BF16)[None]

    span = span_index[0]
    inner_span = lax.dynamic_index_in_dim(inner_params[0], span, 0, keepdims=False).astype(F32)
    base_span = lax.dynamic_index_in_dim(outer_base, span, 0, keepdims=False)
    momentum_span = lax.dynamic_index_in_dim(outer_momentum, span, 0, keepdims=False)
    frag_rows, frag_cols = base_span.shape
    pseudo_delta = (base_span - inner_span).reshape(frag_rows, frag_cols // GROUP, GROUP)
    block_scale = (jnp.max(jnp.abs(pseudo_delta), axis=2) + 1e-06).astype(BF16)
    wide_scale = block_scale.astype(F32)[:, :, None]
    code_values = (pseudo_delta / wide_scale).astype(BF16)
    decoded = (code_values.astype(F32) * wide_scale).astype(BF16).reshape(frag_rows, frag_cols)
    other = lax.ppermute(after(decoded, *in_sent), "replica", [(0, 1), (1, 0)])
    mean_delta = (decoded.astype(F32) + other.astype(F32)) / 2
    new_momentum = outer_decay * momentum_span + mean_delta
    new_base = base_span - outer_rate * (mean_delta + outer_decay * new_momentum)
    return (layer_out, grad_input, grad_gate, grad_up, grad_down, new_base, new_momentum)


def solution(mesh):
    return jax.shard_map(
        body,
        mesh=mesh,
        in_specs=(
            P(("replica", "tpa"), "tpb"),
            P("replica", "tpb", "tpa"),
            P("replica", "tpb", "tpa"),
            P("replica", "tpa", "tpb"),
            P(("replica", "tpa"), "tpb"),
            P("replica", None, "tpa", "tpb"),
            P(None, "tpa", "tpb"),
            P(None, "tpa", "tpb"),
            P(),
        ),
        out_specs=(
            P(("replica", "tpa"), "tpb"),
            P(("replica", "tpa"), "tpb"),
            P("replica", "tpb", "tpa"),
            P("replica", "tpb", "tpa"),
            P("replica", "tpa", "tpb"),
            P("tpa", "tpb"),
            P("tpa", "tpb"),
        ),
        check_vma=False,
    )
```

```python
import jax
import jax.numpy as jnp
from jax import lax
from jax.sharding import PartitionSpec as P

GROUP = 128
outer_rate = 0.7
outer_decay = 0.9
F32 = jnp.float32
BF16 = jnp.bfloat16
TURNED = (((1,), (1,)), ((), ()))


def shift_x(values, step):
    return lax.ppermute(values, "tpa", [(i, (i // 4 + step) % 4 * 4 + i % 4) for i in range(16)])


def shift_z(values, step):
    return lax.ppermute(values, "tpa", [(i, i // 4 * 4 + (i + step) % 4) for i in range(16)])


def shift_y(values, step):
    return lax.ppermute(values, "tpb", [(i, (i // 2 + step) % 4 * 2 + i % 2) for i in range(8)])


def shift_sides(values):
    return lax.ppermute(values, "tpb", [(i, (i // 2 + 1 + 2 * (i % 2)) % 4 * 2 + i % 2) for i in range(8)])


def swap_core(values):
    return lax.ppermute(values, "tpb", [(i, i ^ 1) for i in range(8)])


def after(values, *earlier):
    return lax.optimization_barrier((values,) + earlier)[0]


def add(*terms):
    total = terms[0].astype(F32)
    for term in terms[1:]:
        total = total + term.astype(F32)
    return total


def gather_near(first, second):
    joined = jnp.concatenate([first, second], axis=0)
    parts = [joined] + [shift_z(joined, -dz) for dz in (1, 2, 3)]
    rows = first.shape[0]
    return (
        jnp.concatenate([part[:rows] for part in parts], axis=0),
        jnp.concatenate([part[rows:] for part in parts], axis=0),
    )


def gather_far(near):
    return [near, shift_x(near, -1), shift_x(near, 1), shift_x(near, 2)]


def block(rows, index):
    return lax.dynamic_slice_in_dim(rows, lax.rem(index, 4) * 128, 128, 0)


def half_block(rows, index, core):
    return lax.dynamic_slice_in_dim(rows, lax.rem(index, 4) * 128 + core * 64, 64, 0)


def trade_cores(partial, place, core):
    near = place + 3 + 2 * core
    return jnp.concatenate(
        [
            block(partial, near),
            half_block(partial, place + 2, 1 - core),
            half_block(partial, place, 1 - core),
        ],
        axis=0,
    )


def relay_sends(partial, got, place, core):
    return add(half_block(partial, place + 2, core), got[128:192]).astype(BF16)


def side_sends(partial, got, relayed, place, core):
    near = add(block(partial, place + 1 + 2 * core), got[:128]).reshape(2, 64, partial.shape[1])
    mine = (jnp.arange(2) == core)[:, None, None]
    return (near + jnp.where(mine, relayed.astype(F32)[None], 0)).astype(BF16).reshape(got[:128].shape)


def scatter_sum(partial, got, kept, given, place, core):
    return add(half_block(partial, place, core), got[192:], kept, given)


def split_cores(beside, core):
    return (
        lax.dynamic_slice_in_dim(beside, core * 64, 64, 0),
        lax.dynamic_slice_in_dim(beside, (1 - core) * 64, 64, 0),
    )


def pair_cores(own, sibling, core):
    first = core == 0
    return jnp.concatenate([jnp.where(first, own, sibling), jnp.where(first, sibling, own)], axis=0)


def full_rows(own, sibling, beside, across, other_beside, other_across, core):
    first = core == 0
    above = jnp.where(first, other_beside, beside)
    below = jnp.where(first, beside, other_beside)
    above_mine, above_other = split_cores(above, core)
    below_mine, below_other = split_cores(below, core)
    return jnp.concatenate(
        [own, above_mine, across, below_mine, sibling, above_other, other_across, below_other], axis=0
    )


def turn_rows(rows, place, core):
    grid = rows.reshape(4, 2, 64, rows.shape[1])
    grid = lax.dynamic_slice_in_dim(jnp.concatenate([grid, grid], axis=0), place, 4, 0)
    grid = lax.dynamic_slice_in_dim(jnp.concatenate([grid, grid], axis=1), core, 2, 1)
    return grid.transpose(1, 0, 2, 3).reshape(rows.shape)


def far_block(rows, index, place):
    start = lax.rem(index + 4 - place, 4) * 64
    return jnp.concatenate(
        [lax.dynamic_slice_in_dim(rows, start, 64, 0), lax.dynamic_slice_in_dim(rows, start + 256, 64, 0)], axis=0
    )


def shift_far(parts):
    return [shift_x(parts[0], 2), shift_x(parts[1], 1), shift_x(parts[2], -1)]


def shift_near(line, core):
    sent = line.astype(BF16)

    def part(rows, dz):
        start = jnp.bitwise_xor(core, dz // 2) * 64 + dz % 2 * 32
        return lax.dynamic_slice_in_dim(rows, start, 32, 0)

    return [part(line, 0)] + [shift_z(part(sent, dz), dz) for dz in (1, 2, 3)]


def body(
    layer_input,
    gate_weight,
    up_weight,
    down_weight,
    out_grad,
    inner_params,
    outer_base,
    outer_momentum,
    span_index,
):
    w_both = lax.optimization_barrier(jnp.concatenate([gate_weight[0], up_weight[0]], axis=1))
    w_down = down_weight[0]
    width = w_down.shape[0]
    place = lax.axis_index("tpb") // 2
    core = lax.axis_index("tpb") % 2

    span = span_index[0]
    inner_span = lax.dynamic_index_in_dim(inner_params[0], span, 0, keepdims=False).astype(F32)
    base_span = lax.dynamic_index_in_dim(outer_base, span, 0, keepdims=False)
    momentum_span = lax.dynamic_index_in_dim(outer_momentum, span, 0, keepdims=False)
    frag_rows, frag_cols = base_span.shape
    pseudo_delta = (base_span - inner_span).reshape(frag_rows, frag_cols // GROUP, GROUP)
    block_scale = (jnp.max(jnp.abs(pseudo_delta), axis=2) + 1e-06).astype(BF16)
    wide_scale = block_scale.astype(F32)[:, :, None]
    code_values = (pseudo_delta / wide_scale).astype(BF16)
    decoded = (code_values.astype(F32) * wide_scale).astype(BF16).reshape(frag_rows, frag_cols)

    near_in, near_grad = gather_near(layer_input, out_grad)
    rows_in = jnp.concatenate(gather_far(near_in), axis=0)
    blocks_grad = gather_far(after(near_grad, near_in))

    projected = jnp.dot(rows_in, w_both, preferred_element_type=F32).astype(BF16)
    traded = swap_core(trade_cores(projected, place, core))
    relayed = shift_sides(relay_sends(projected, traded, place, core))
    relayed = after(relayed, *blocks_grad[1:3])
    beside = shift_sides(side_sends(projected, traded, relayed, place, core))
    kept, given = split_cores(beside, core)
    gate_up = scatter_sum(projected, traded, kept, swap_core(given), place, core)
    gate_sum = gate_up[:, :width]
    up_sum = gate_up[:, width:]
    sigmoid_gate = jax.nn.sigmoid(gate_sum)
    activated = gate_sum * sigmoid_gate
    hidden_part = (activated * up_sum).astype(BF16)
    silu_slope = sigmoid_gate * (1.0 + gate_sum * (1.0 - sigmoid_gate))

    grad_rows = jnp.concatenate([after(part, beside) for part in blocks_grad], axis=0)
    back = lax.dot_general(grad_rows, w_down, TURNED, preferred_element_type=F32).astype(BF16)
    back_traded = swap_core(trade_cores(back, place, core))
    back_relay = relay_sends(back, back_traded, place, core)
    hidden_sibling = swap_core(hidden_part)
    hidden_pair = pair_cores(hidden_part, hidden_sibling, core)
    first_got = shift_sides(jnp.concatenate([back_relay, hidden_pair], axis=0))
    back_beside = side_sends(back, back_traded, first_got[:64], place, core)
    hidden_beside = first_got[64:]
    hidden_onward, _ = split_cores(hidden_beside, core)
    second_got = shift_sides(jnp.concatenate([back_beside, hidden_onward], axis=0))

    other_decoded = lax.ppermute(after(decoded, hidden_pair), "replica", [(0, 1), (1, 0)])
    rows_turned = lax.optimization_barrier(turn_rows(rows_in, place, core).T)
    grad_ordered = lax.optimization_barrier(turn_rows(grad_rows, place, core))
    second_got = after(second_got, other_decoded, rows_turned, grad_ordered)

    kept, given = split_cores(second_got[:128], core)
    hidden_across = second_got[128:]
    swapped = swap_core(jnp.concatenate([given, hidden_beside, hidden_across], axis=0))
    hidden_grad = scatter_sum(back, back_traded, kept, swapped[:64], place, core)
    hidden_full = full_rows(
        hidden_part, hidden_sibling, hidden_beside, hidden_across, swapped[64:192], swapped[192:], core
    )

    grad_part = jnp.concatenate(
        [(hidden_grad * up_sum * silu_slope).astype(BF16), (hidden_grad * activated).astype(BF16)], axis=1
    )
    grad_sibling = swap_core(grad_part)
    grad_pair = pair_cores(grad_part, grad_sibling, core)
    grad_beside = shift_sides(grad_pair)
    hidden_full = after(hidden_full, grad_pair)
    out_partial = jnp.dot(hidden_full, w_down, preferred_element_type=F32).astype(BF16)
    out_parts = lax.optimization_barrier([far_block(out_partial, k, place) for k in (3, 1, 2, 0)])
    out_got = shift_far(out_parts)
    grad_beside = after(grad_beside, *out_parts)
    grad_onward, _ = split_cores(grad_beside, core)
    grad_across = shift_sides(grad_onward)
    grad_swapped = swap_core(jnp.concatenate([grad_beside, grad_across], axis=0))
    grad_hidden = full_rows(
        grad_part, grad_sibling, grad_beside, grad_across, grad_swapped[:128], grad_swapped[128:], core
    )
    in_partial = lax.dot_general(grad_hidden, w_both, TURNED, preferred_element_type=F32).astype(BF16)
    in_parts = lax.optimization_barrier([far_block(in_partial, k, place) for k in (3, 1, 2, 0)])

    in_got = shift_far(in_parts)
    out_line = add(*after(out_got, *in_parts), out_parts[3])
    out_near = shift_near(after(out_line, in_got[1]), core)
    layer_out = add(layer_input, *out_near).astype(BF16)
    in_line = add(*in_got, in_parts[3])
    in_near = shift_near(after(in_line, out_near[1]), core)
    grad_input = add(out_grad, *in_near).astype(BF16)

    hidden_last, grad_last = after((hidden_full, grad_hidden), *out_got, *in_parts)
    grad_down = lax.dot_general(
        hidden_last, grad_ordered, (((0,), (0,)), ((), ())), preferred_element_type=F32
    ).astype(BF16)[None]
    grad_gate = jnp.dot(rows_turned, grad_last[:, :width], preferred_element_type=F32).astype(BF16)[None]
    grad_last = after(grad_last, in_near[1])
    grad_up = jnp.dot(rows_turned, grad_last[:, width:], preferred_element_type=F32).astype(BF16)[None]

    mean_delta = (decoded.astype(F32) + other_decoded.astype(F32)) / 2
    new_momentum = outer_decay * momentum_span + mean_delta
    new_base = base_span - outer_rate * (mean_delta + outer_decay * new_momentum)
    return (layer_out, grad_input, grad_gate, grad_up, grad_down, new_base, new_momentum)


def solution(mesh):
    return jax.shard_map(
        body,
        mesh=mesh,
        in_specs=(
            P(("replica", "tpa"), "tpb"),
            P("replica", "tpb", "tpa"),
            P("replica", "tpb", "tpa"),
            P("replica", "tpa", "tpb"),
            P(("replica", "tpa"), "tpb"),
            P("replica", None, "tpa", "tpb"),
            P(None, "tpa", "tpb"),
            P(None, "tpa", "tpb"),
            P(),
        ),
        out_specs=(
            P(("replica", "tpa"), "tpb"),
            P(("replica", "tpa"), "tpb"),
            P("replica", "tpb", "tpa"),
            P("replica", "tpb", "tpa"),
            P("replica", "tpa", "tpb"),
            P("tpa", "tpb"),
            P("tpa", "tpb"),
        ),
        check_vma=False,
    )
```

```python
import jax
import jax.numpy as jnp
from jax import lax
from jax.sharding import PartitionSpec as P

GROUP = 128
outer_rate = 0.7
outer_decay = 0.9
F32 = jnp.float32
BF16 = jnp.bfloat16
TURNED = (((1,), (1,)), ((), ()))


def shift_x(values, step):
    return lax.ppermute(values, "tpa", [(i, (i // 4 + step) % 4 * 4 + i % 4) for i in range(16)])


def shift_z(values, step):
    return lax.ppermute(values, "tpa", [(i, i // 4 * 4 + (i + step) % 4) for i in range(16)])


def shift_y(values, step):
    return lax.ppermute(values, "tpb", [(i, (i // 2 + step) % 4 * 2 + i % 2) for i in range(8)])


def shift_sides(values):
    return lax.ppermute(values, "tpb", [(i, (i // 2 + 1 + 2 * (i % 2)) % 4 * 2 + i % 2) for i in range(8)])


def swap_core(values):
    return lax.ppermute(values, "tpb", [(i, i ^ 1) for i in range(8)])


def together(*arrays):
    return lax.optimization_barrier(arrays)


def add(*terms):
    total = terms[0].astype(F32)
    for term in terms[1:]:
        total = total + term.astype(F32)
    return total


def gather_near(first, second):
    joined = jnp.concatenate([first, second], axis=0)
    parts = [joined] + [shift_z(joined, -dz) for dz in (1, 2, 3)]
    rows = first.shape[0]
    return (
        jnp.concatenate([part[:rows] for part in parts], axis=0),
        jnp.concatenate([part[rows:] for part in parts], axis=0),
    )


def gather_far(near):
    return [near, shift_x(near, -1), shift_x(near, 1), shift_x(near, 2)]


def places(index):
    index = index.astype(jnp.uint32)
    core = index & 1
    place = lax.shift_right_logical(index, jnp.uint32(1))
    near = (place + 1 + 2 * core) & 3
    opposite = ((place + 2) & 3) * 128
    return {
        "place": place,
        "core": core,
        "near": near * 128,
        "other_near": ((near + 2) & 3) * 128,
        "across": opposite + core * 64,
        "other_across": opposite + 64 - core * 64,
        "own": place * 128 + core * 64,
        "other_own": place * 128 + 64 - core * 64,
        "kept": core * 64,
        "given": 64 - core * 64,
        "far": [((k + 4 - place) & 3) * 64 for k in range(4)],
        "far_other": [((k + 4 - place) & 3) * 64 + 256 for k in range(4)],
        "line": [(core ^ (dz // 2)) * 64 + dz % 2 * 32 for dz in range(4)],
    }


def rows_at(values, start, count):
    return lax.dynamic_slice(values, (start, jnp.uint32(0)), (count, values.shape[1]))


def trade_cores(partials, at):
    def rows(partial):
        return jnp.concatenate(
            [
                rows_at(partial, at["other_near"], 128),
                rows_at(partial, at["other_across"], 64),
                rows_at(partial, at["other_own"], 64),
            ],
            axis=0,
        )

    return jnp.concatenate([rows(partial) for partial in partials], axis=1)


def columns(values, count):
    width = values.shape[1] // count
    return [values[:, k * width : (k + 1) * width] for k in range(count)]


def scatter_sends(partials, got, at):
    pairs = list(zip(partials, columns(got, len(partials))))
    beside = [add(rows_at(partial, at["near"], 128), part[:128]).astype(BF16) for partial, part in pairs]
    across = [add(rows_at(partial, at["across"], 64), part[128:192]).astype(BF16) for partial, part in pairs]
    return jnp.concatenate(beside, axis=1), jnp.concatenate(across, axis=1)


def scatter_sum(partials, got, across, kept, given, at):
    count = len(partials)
    parts = zip(partials, *[columns(v, count) for v in (got, across, kept, given)])
    return [add(rows_at(p, at["own"], 64), g[192:], a, k, o) for p, g, a, k, o in parts]


def split_cores(beside, at):
    return rows_at(beside, at["kept"], 64), rows_at(beside, at["given"], 64)


def pair_cores(own, sibling, first):
    return jnp.concatenate([jnp.where(first, own, sibling), jnp.where(first, sibling, own)], axis=0)


def full_rows(own, sibling, beside, across, other_beside, other_across, at):
    first = at["first"]
    above = jnp.where(first, other_beside, beside)
    below = jnp.where(first, beside, other_beside)
    above_mine, above_other = split_cores(above, at)
    below_mine, below_other = split_cores(below, at)
    return jnp.concatenate(
        [own, above_mine, across, below_mine, sibling, above_other, other_across, below_other], axis=0
    )


def turn_rows(rows, at):
    zero = jnp.uint32(0)
    grid = rows.reshape(4, 2, 64, rows.shape[1])
    grid = lax.dynamic_slice(jnp.concatenate([grid, grid], axis=0), (at["place"], zero, zero, zero), grid.shape)
    grid = lax.dynamic_slice(jnp.concatenate([grid, grid], axis=1), (zero, at["core"], zero, zero), grid.shape)
    return grid.transpose(1, 0, 2, 3).reshape(rows.shape)


def far_block(rows, index, at):
    return jnp.concatenate(
        [rows_at(rows, at["far"][index], 64), rows_at(rows, at["far_other"][index], 64)], axis=0
    )


def shift_far(parts):
    return [shift_x(parts[0], 2), shift_x(parts[1], 1), shift_x(parts[2], -1)]


def shift_near(line, at):
    sent = line.astype(BF16)
    return [rows_at(line, at["line"][0], 32)] + [
        shift_z(rows_at(sent, at["line"][dz], 32), dz) for dz in (1, 2, 3)
    ]


def take_span(values, span):
    zero = jnp.uint32(0)
    return lax.dynamic_slice(values, (span, zero, zero), (1,) + values.shape[1:])[0]


def body(
    layer_input,
    gate_weight,
    up_weight,
    down_weight,
    out_grad,
    inner_params,
    outer_base,
    outer_momentum,
    span_index,
):
    w_gate = gate_weight[0]
    w_up = up_weight[0]
    w_down = down_weight[0]
    width = w_down.shape[0]
    span = span_index[0].astype(jnp.uint32)
    at = places(lax.axis_index("tpb"))
    at["first"] = at["core"] == 0
    layer_input, out_grad, at, span = together(layer_input, out_grad, at, span)

    inner_span = take_span(inner_params[0], span).astype(F32)
    base_span = take_span(outer_base, span)
    momentum_span = take_span(outer_momentum, span)
    frag_rows, frag_cols = base_span.shape
    pseudo_delta = (base_span - inner_span).reshape(frag_rows, frag_cols // GROUP, GROUP)
    block_scale = (jnp.max(jnp.abs(pseudo_delta), axis=2) + 1e-06).astype(BF16)
    wide_scale = block_scale.astype(F32)[:, :, None]
    code_values = (pseudo_delta / wide_scale).astype(BF16)
    decoded = (code_values.astype(F32) * wide_scale).astype(BF16).reshape(frag_rows, frag_cols)

    near_in, near_grad = gather_near(layer_input, out_grad)
    rows_in = jnp.concatenate(gather_far(near_in), axis=0)
    blocks_grad = gather_far(near_grad)

    projected = [jnp.dot(rows_in, w, preferred_element_type=F32).astype(BF16) for w in (w_gate, w_up)]
    traded = swap_core(trade_cores(projected, at))
    beside, across = scatter_sends(projected, traded, at)
    beside, across, *blocks_grad = together(shift_sides(beside), shift_y(across, 2), *blocks_grad)
    kept, given = split_cores(beside, at)
    gate_sum, up_sum = scatter_sum(projected, traded, across, kept, swap_core(given), at)
    sigmoid_gate = jax.nn.sigmoid(gate_sum)
    activated = gate_sum * sigmoid_gate
    hidden_part = (activated * up_sum).astype(BF16)
    silu_slope = sigmoid_gate * (1.0 + gate_sum * (1.0 - sigmoid_gate))

    grad_rows = jnp.concatenate(blocks_grad, axis=0)
    back = [lax.dot_general(grad_rows, w_down, TURNED, preferred_element_type=F32).astype(BF16)]
    back_traded = swap_core(trade_cores(back, at))
    back_beside, back_across = scatter_sends(back, back_traded, at)
    hidden_sibling = swap_core(hidden_part)
    hidden_pair = pair_cores(hidden_part, hidden_sibling, at["first"])
    beside = shift_sides(jnp.concatenate([back_beside, hidden_pair], axis=0))
    across = shift_y(jnp.concatenate([back_across, hidden_part], axis=0), 2)

    decoded, hidden_kept = together(decoded, hidden_part)
    other_decoded = lax.ppermute(decoded, "replica", [(0, 1), (1, 0)])
    rows_turned = lax.optimization_barrier(turn_rows(rows_in, at).T)
    grad_ordered = lax.optimization_barrier(turn_rows(grad_rows, at))
    beside, across, other_decoded, rows_turned, grad_ordered = together(
        beside, across, other_decoded, rows_turned, grad_ordered
    )

    kept, given = split_cores(beside[:128], at)
    swapped = swap_core(jnp.concatenate([given, beside[128:], across[64:]], axis=0))
    (hidden_grad,) = scatter_sum(back, back_traded, across[:64], kept, swapped[:64], at)
    hidden_full = full_rows(
        hidden_kept, hidden_sibling, beside[128:], across[64:], swapped[64:192], swapped[192:], at
    )

    grad_part = jnp.concatenate(
        [(hidden_grad * up_sum * silu_slope).astype(BF16), (hidden_grad * activated).astype(BF16)], axis=1
    )
    grad_sibling = swap_core(grad_part)
    grad_pair = pair_cores(grad_part, grad_sibling, at["first"])
    grad_beside = shift_sides(grad_pair)
    grad_across = shift_y(grad_part, 2)
    out_partial = jnp.dot(hidden_full, w_down, preferred_element_type=F32).astype(BF16)
    *out_parts, out_own = together(*[far_block(out_partial, k, at) for k in (3, 1, 2, 0)])
    out_got = shift_far(out_parts)
    grad_beside, grad_across, *out_got[1:] = together(grad_beside, grad_across, *out_got[1:])
    grad_swapped = swap_core(jnp.concatenate([grad_beside, grad_across], axis=0))
    grad_hidden = full_rows(
        grad_part, grad_sibling, grad_beside, grad_across, grad_swapped[:128], grad_swapped[128:], at
    )
    in_partial = add(
        lax.dot_general(grad_hidden[:, :width], w_gate, TURNED, preferred_element_type=F32),
        lax.dot_general(grad_hidden[:, width:], w_up, TURNED, preferred_element_type=F32),
    ).astype(BF16)
    *in_parts, in_own = together(*[far_block(in_partial, k, at) for k in (3, 1, 2, 0)])
    in_got = shift_far(in_parts)

    hidden_full, grad_hidden, in_own = together(hidden_full, grad_hidden, in_own)
    grad_down = lax.dot_general(
        hidden_full, grad_ordered, (((0,), (0,)), ((), ())), preferred_element_type=F32
    ).astype(BF16)[None]
    grad_gate_h, grad_up_h = columns(grad_hidden, 2)
    grad_gate = jnp.dot(rows_turned, grad_gate_h, preferred_element_type=F32).astype(BF16)[None]
    out_got[0], in_got[1] = together(out_got[0], in_got[1])
    out_line = add(*out_got, out_own)
    out_near = shift_near(out_line, at)
    in_line, out_near[1] = together(add(*in_got, in_own), out_near[1])
    in_near = shift_near(in_line, at)
    grad_up_h, in_near[1] = together(grad_up_h, in_near[1])
    grad_up = jnp.dot(rows_turned, grad_up_h, preferred_element_type=F32).astype(BF16)[None]
    layer_out = add(layer_input, *out_near).astype(BF16)
    grad_input = add(out_grad, *in_near).astype(BF16)

    mean_delta = (decoded.astype(F32) + other_decoded.astype(F32)) / 2
    new_momentum = outer_decay * momentum_span + mean_delta
    new_base = base_span - outer_rate * (mean_delta + outer_decay * new_momentum)
    return (layer_out, grad_input, grad_gate, grad_up, grad_down, new_base, new_momentum)


def solution(mesh):
    return jax.shard_map(
        body,
        mesh=mesh,
        in_specs=(
            P(("replica", "tpa"), "tpb"),
            P("replica", "tpb", "tpa"),
            P("replica", "tpb", "tpa"),
            P("replica", "tpa", "tpb"),
            P(("replica", "tpa"), "tpb"),
            P("replica", None, "tpa", "tpb"),
            P(None, "tpa", "tpb"),
            P(None, "tpa", "tpb"),
            P(),
        ),
        out_specs=(
            P(("replica", "tpa"), "tpb"),
            P(("replica", "tpa"), "tpb"),
            P("replica", "tpb", "tpa"),
            P("replica", "tpb", "tpa"),
            P("replica", "tpa", "tpb"),
            P("tpa", "tpb"),
            P("tpa", "tpb"),
        ),
        check_vma=False,
    )
```

```python
import jax
import jax.numpy as jnp
from jax import lax
from jax.sharding import PartitionSpec as P

GROUP = 128
outer_rate = 0.7
outer_decay = 0.9
F32 = jnp.float32
BF16 = jnp.bfloat16
TURNED = (((1,), (1,)), ((), ()))


def shift_x(values, step):
    return lax.ppermute(values, "tpa", [(i, (i // 4 + step) % 4 * 4 + i % 4) for i in range(16)])


def shift_z(values, step):
    return lax.ppermute(values, "tpa", [(i, i // 4 * 4 + (i + step) % 4) for i in range(16)])


def shift_y(values, step):
    return lax.ppermute(values, "tpb", [(i, (i // 2 + step) % 4 * 2 + i % 2) for i in range(8)])


def shift_sides(values):
    return lax.ppermute(values, "tpb", [(i, (i // 2 + 1 + 2 * (i % 2)) % 4 * 2 + i % 2) for i in range(8)])


def swap_core(values):
    return lax.ppermute(values, "tpb", [(i, i ^ 1) for i in range(8)])


def together(*arrays):
    return lax.optimization_barrier(arrays)


def add(*terms):
    total = terms[0].astype(F32)
    for term in terms[1:]:
        total = total + term.astype(F32)
    return total


def near_parts(values):
    return [values] + [shift_z(values, -dz) for dz in (1, 2, 3)]


def gather_far(near):
    return [near, shift_x(near, -1), shift_x(near, 1), shift_x(near, 2)]


def places(index):
    index = index.astype(jnp.uint32)
    core = index & 1
    place = lax.shift_right_logical(index, jnp.uint32(1))
    near = (place + 1 + 2 * core) & 3
    opposite = ((place + 2) & 3) * 128
    return {
        "place": place,
        "core": core,
        "near": near * 128,
        "other_near": ((near + 2) & 3) * 128,
        "across": opposite + core * 64,
        "other_across": opposite + 64 - core * 64,
        "own": place * 128 + core * 64,
        "other_own": place * 128 + 64 - core * 64,
        "far": [((k + 4 - place) & 3) * 64 for k in range(4)],
        "far_other": [((k + 4 - place) & 3) * 64 + 256 for k in range(4)],
        "line": [(core ^ (dz // 2)) * 64 + dz % 2 * 32 for dz in range(4)],
    }


def rows_at(values, start, count):
    return lax.dynamic_slice(values, (start, jnp.uint32(0)), (count, values.shape[1]))


def trade_cores(partials, at):
    def rows(partial):
        return jnp.concatenate(
            [
                rows_at(partial, at["other_near"], 128),
                rows_at(partial, at["other_across"], 64),
                rows_at(partial, at["other_own"], 64),
            ],
            axis=0,
        )

    return jnp.concatenate([rows(partial) for partial in partials], axis=1)


def columns(values, count):
    width = values.shape[1] // count
    return [values[:, k * width : (k + 1) * width] for k in range(count)]


def scatter_sends(partials, got, at):
    pairs = list(zip(partials, columns(got, len(partials))))
    beside = [add(rows_at(partial, at["near"], 128), part[:128]).astype(BF16) for partial, part in pairs]
    across = [add(rows_at(partial, at["across"], 64), part[128:192]).astype(BF16) for partial, part in pairs]
    return jnp.concatenate(beside, axis=1), jnp.concatenate(across, axis=1)


def scatter_sum(partials, got, across, kept, given, at):
    count = len(partials)
    parts = zip(partials, *[columns(v, count) for v in (got, across, kept, given)])
    return [add(rows_at(p, at["own"], 64), g[192:], a, k, o) for p, g, a, k, o in parts]


def split_cores(beside, at):
    low, high = beside[:64], beside[64:]
    return jnp.where(at["first"], low, high), jnp.where(at["first"], high, low)


def pair_cores(own, sibling, first):
    return jnp.concatenate([jnp.where(first, own, sibling), jnp.where(first, sibling, own)], axis=0)


def full_rows(own, sibling, beside, across, other_beside, other_across, at):
    first = at["first"]
    above = jnp.where(first, other_beside, beside)
    below = jnp.where(first, beside, other_beside)
    above_mine, above_other = split_cores(above, at)
    below_mine, below_other = split_cores(below, at)
    return jnp.concatenate(
        [own, above_mine, across, below_mine, sibling, above_other, other_across, below_other], axis=0
    )


def turn_rows(rows, at):
    zero = jnp.uint32(0)
    grid = rows.reshape(4, 2, 64, rows.shape[1])
    grid = lax.dynamic_slice(jnp.concatenate([grid, grid], axis=0), (at["place"], zero, zero, zero), grid.shape)
    grid = lax.dynamic_slice(jnp.concatenate([grid, grid], axis=1), (zero, at["core"], zero, zero), grid.shape)
    return grid.transpose(1, 0, 2, 3).reshape(rows.shape)


def far_block(rows, index, at):
    return jnp.concatenate(
        [rows_at(rows, at["far"][index], 64), rows_at(rows, at["far_other"][index], 64)], axis=0
    )


def shift_far(parts):
    return [shift_x(parts[0], 2), shift_x(parts[1], 1), shift_x(parts[2], -1)]


def shift_near(line, at):
    sent = line.astype(BF16)
    return [rows_at(line, at["line"][0], 32)] + [
        shift_z(rows_at(sent, at["line"][dz], 32), dz) for dz in (1, 2, 3)
    ]


def take_span(values, span):
    zero = jnp.uint32(0)
    return lax.dynamic_slice(values, (span, zero, zero), (1,) + values.shape[1:])[0]


def body(
    layer_input,
    gate_weight,
    up_weight,
    down_weight,
    out_grad,
    inner_params,
    outer_base,
    outer_momentum,
    span_index,
):
    w_gate = gate_weight[0]
    w_up = up_weight[0]
    w_down = down_weight[0]
    width = w_down.shape[0]
    span = span_index[0].astype(jnp.uint32)
    at = places(lax.axis_index("tpb"))
    at["first"] = at["core"] == 0
    layer_input, out_grad, at, span = together(layer_input, out_grad, at, span)

    inner_span = take_span(inner_params[0], span).astype(F32)
    base_span = take_span(outer_base, span)
    momentum_span = take_span(outer_momentum, span)
    frag_rows, frag_cols = base_span.shape
    pseudo_delta = (base_span - inner_span).reshape(frag_rows, frag_cols // GROUP, GROUP)
    block_scale = (jnp.max(jnp.abs(pseudo_delta), axis=2) + 1e-06).astype(BF16)
    wide_scale = block_scale.astype(F32)[:, :, None]
    code_values = (pseudo_delta / wide_scale).astype(BF16)
    decoded = (code_values.astype(F32) * wide_scale).astype(BF16).reshape(frag_rows, frag_cols)

    blocks_in = gather_far(jnp.concatenate(near_parts(layer_input), axis=0))
    parts_grad = near_parts(out_grad)
    arrived = together(*blocks_in[1:], *parts_grad[1:])
    rows_in = jnp.concatenate(blocks_in[:1] + list(arrived[:3]), axis=0)
    blocks_grad = gather_far(jnp.concatenate(parts_grad[:1] + list(arrived[3:]), axis=0))

    projected = [jnp.dot(rows_in, w, preferred_element_type=F32).astype(BF16) for w in (w_gate, w_up)]
    traded = swap_core(trade_cores(projected, at))
    beside, across = scatter_sends(projected, traded, at)
    beside, across, *blocks_grad = together(shift_sides(beside), shift_y(across, 2), *blocks_grad)
    kept, given = split_cores(beside, at)
    gate_sum, up_sum = scatter_sum(projected, traded, across, kept, swap_core(given), at)
    sigmoid_gate = jax.nn.sigmoid(gate_sum)
    activated = gate_sum * sigmoid_gate
    hidden_part = (activated * up_sum).astype(BF16)
    silu_slope = sigmoid_gate * (1.0 + gate_sum * (1.0 - sigmoid_gate))

    grad_rows = jnp.concatenate(blocks_grad, axis=0)
    back = [lax.dot_general(grad_rows, w_down, TURNED, preferred_element_type=F32).astype(BF16)]
    back_traded = swap_core(trade_cores(back, at))
    back_beside, back_across = scatter_sends(back, back_traded, at)
    hidden_sibling = swap_core(hidden_part)
    hidden_pair = pair_cores(hidden_part, hidden_sibling, at["first"])
    beside = shift_sides(jnp.concatenate([back_beside, hidden_pair], axis=0))
    across = shift_y(jnp.concatenate([back_across, hidden_part], axis=0), 2)

    decoded, hidden_kept = together(decoded, hidden_part)
    other_decoded = lax.ppermute(decoded, "replica", [(0, 1), (1, 0)])
    rows_turned = lax.optimization_barrier(turn_rows(rows_in, at).T)
    grad_ordered = lax.optimization_barrier(turn_rows(grad_rows, at))
    beside, across, other_decoded, rows_turned, grad_ordered = together(
        beside, across, other_decoded, rows_turned, grad_ordered
    )

    kept, given = split_cores(beside[:128], at)
    swapped = swap_core(jnp.concatenate([given, beside[128:], across[64:]], axis=0))
    (hidden_grad,) = scatter_sum(back, back_traded, across[:64], kept, swapped[:64], at)
    hidden_full = full_rows(
        hidden_kept, hidden_sibling, beside[128:], across[64:], swapped[64:192], swapped[192:], at
    )

    grad_part = jnp.concatenate(
        [(hidden_grad * up_sum * silu_slope).astype(BF16), (hidden_grad * activated).astype(BF16)], axis=1
    )
    grad_sibling = swap_core(grad_part)
    grad_pair = pair_cores(grad_part, grad_sibling, at["first"])
    grad_beside = shift_sides(grad_pair)
    grad_across = shift_y(grad_part, 2)
    out_partial = jnp.dot(hidden_full, w_down, preferred_element_type=F32).astype(BF16)
    *out_parts, out_own = together(*[far_block(out_partial, k, at) for k in (3, 1, 2, 0)])
    out_got = shift_far(out_parts)
    grad_down = lax.dot_general(
        hidden_full, grad_ordered, (((0,), (0,)), ((), ())), preferred_element_type=F32
    ).astype(BF16)[None]
    grad_beside, grad_across, grad_down, *out_got = together(grad_beside, grad_across, grad_down, *out_got)
    grad_swapped = swap_core(jnp.concatenate([grad_beside, grad_across], axis=0))
    grad_hidden = full_rows(
        grad_part, grad_sibling, grad_beside, grad_across, grad_swapped[:128], grad_swapped[128:], at
    )
    in_partial = add(
        lax.dot_general(grad_hidden[:, :width], w_gate, TURNED, preferred_element_type=F32),
        lax.dot_general(grad_hidden[:, width:], w_up, TURNED, preferred_element_type=F32),
    ).astype(BF16)
    *in_parts, in_own = together(*[far_block(in_partial, k, at) for k in (3, 1, 2, 0)])
    in_got = shift_far(in_parts)

    grad_hidden, in_own = together(grad_hidden, in_own)
    grad_gate, grad_up = [
        jnp.dot(rows_turned, part, preferred_element_type=F32).astype(BF16)[None]
        for part in columns(grad_hidden, 2)
    ]
    out_got[0], in_got[1] = together(out_got[0], in_got[1])
    out_near = shift_near(add(*out_got, out_own), at)
    in_line, out_near[1] = together(add(*in_got, in_own), out_near[1])
    in_near = shift_near(in_line, at)
    layer_out = add(layer_input, *out_near).astype(BF16)
    grad_input = add(out_grad, *in_near).astype(BF16)

    mean_delta = (decoded.astype(F32) + other_decoded.astype(F32)) / 2
    new_momentum = outer_decay * momentum_span + mean_delta
    new_base = base_span - outer_rate * (mean_delta + outer_decay * new_momentum)
    return (layer_out, grad_input, grad_gate, grad_up, grad_down, new_base, new_momentum)


def solution(mesh):
    return jax.shard_map(
        body,
        mesh=mesh,
        in_specs=(
            P(("replica", "tpa"), "tpb"),
            P("replica", "tpb", "tpa"),
            P("replica", "tpb", "tpa"),
            P("replica", "tpa", "tpb"),
            P(("replica", "tpa"), "tpb"),
            P("replica", None, "tpa", "tpb"),
            P(None, "tpa", "tpb"),
            P(None, "tpa", "tpb"),
            P(),
        ),
        out_specs=(
            P(("replica", "tpa"), "tpb"),
            P(("replica", "tpa"), "tpb"),
            P("replica", "tpb", "tpa"),
            P("replica", "tpb", "tpa"),
            P("replica", "tpa", "tpb"),
            P("tpa", "tpb"),
            P("tpa", "tpb"),
        ),
        check_vma=False,
    )
```

```python
import jax
import jax.numpy as jnp
from jax import lax
from jax.sharding import PartitionSpec as P

GROUP = 128
outer_rate = 0.7
outer_decay = 0.9
F32 = jnp.float32
BF16 = jnp.bfloat16
TURNED = (((1,), (1,)), ((), ()))


def shift_x(values, step):
    return lax.ppermute(values, "tpa", [(i, (i // 4 + step) % 4 * 4 + i % 4) for i in range(16)])


def shift_z(values, step):
    return lax.ppermute(values, "tpa", [(i, i // 4 * 4 + (i + step) % 4) for i in range(16)])


def shift_y(values, step):
    return lax.ppermute(values, "tpb", [(i, (i // 2 + step) % 4 * 2 + i % 2) for i in range(8)])


def shift_sides(values):
    return lax.ppermute(values, "tpb", [(i, (i // 2 + 1 + 2 * (i % 2)) % 4 * 2 + i % 2) for i in range(8)])


def swap_core(values):
    return lax.ppermute(values, "tpb", [(i, i ^ 1) for i in range(8)])


def together(*arrays):
    return lax.optimization_barrier(arrays)


def add(*terms):
    total = terms[0].astype(F32)
    for term in terms[1:]:
        total = total + term.astype(F32)
    return total


def near_parts(values):
    return [values] + [shift_z(values, -dz) for dz in (1, 2, 3)]


def gather_far(near):
    return [near, shift_x(near, -1), shift_x(near, 1), shift_x(near, 2)]


def places(index):
    index = index.astype(jnp.uint32)
    core = index & 1
    place = lax.shift_right_logical(index, jnp.uint32(1))
    near = (place + 1 + 2 * core) & 3
    opposite = ((place + 2) & 3) * 128
    return {
        "place": place,
        "core": core,
        "near": near * 128,
        "other_near": ((near + 2) & 3) * 128,
        "across": opposite + core * 64,
        "other_across": opposite + 64 - core * 64,
        "own": place * 128 + core * 64,
        "other_own": place * 128 + 64 - core * 64,
        "far": [((k + 4 - place) & 3) * 64 for k in range(4)],
        "far_other": [((k + 4 - place) & 3) * 64 + 256 for k in range(4)],
        "line": [(core ^ (dz // 2)) * 64 + dz % 2 * 32 for dz in range(4)],
    }


def rows_at(values, start, count):
    return lax.dynamic_slice(values, (start, jnp.uint32(0)), (count, values.shape[1]))


def trade_cores(partials, at):
    def rows(partial):
        return jnp.concatenate(
            [
                rows_at(partial, at["other_near"], 128),
                rows_at(partial, at["other_across"], 64),
                rows_at(partial, at["other_own"], 64),
            ],
            axis=0,
        )

    return jnp.concatenate([rows(partial) for partial in partials], axis=1)


def columns(values, count):
    width = values.shape[1] // count
    return [values[:, k * width : (k + 1) * width] for k in range(count)]


def scatter_sends(partials, got, at):
    pairs = list(zip(partials, columns(got, len(partials))))
    beside = [add(rows_at(partial, at["near"], 128), part[:128]).astype(BF16) for partial, part in pairs]
    across = [add(rows_at(partial, at["across"], 64), part[128:192]).astype(BF16) for partial, part in pairs]
    return jnp.concatenate(beside, axis=1), jnp.concatenate(across, axis=1)


def scatter_sum(partials, got, across, kept, given, at):
    count = len(partials)
    parts = zip(partials, *[columns(v, count) for v in (got, across, kept, given)])
    return [add(rows_at(p, at["own"], 64), g[192:], a, k, o) for p, g, a, k, o in parts]


def split_cores(beside, at):
    low, high = beside[:64], beside[64:]
    return jnp.where(at["first"], low, high), jnp.where(at["first"], high, low)


def pair_cores(own, sibling, first):
    return jnp.concatenate([jnp.where(first, own, sibling), jnp.where(first, sibling, own)], axis=0)


def paired_rows(own, sibling, beside, across, other_beside, other_across, at):
    first = at["first"]
    above = jnp.where(first, other_beside, beside)
    below = jnp.where(first, beside, other_beside)
    above_mine, above_other = split_cores(above, at)
    below_mine, below_other = split_cores(below, at)
    return jnp.concatenate(
        [own, above_mine, across, below_mine, sibling, above_other, other_across, below_other], axis=0
    )


def ring_blocks(own):
    return [own, shift_y(own, -1), shift_y(own, 2), shift_y(own, 1)]


def ring_rows(blocks):
    mine = jnp.concatenate(blocks, axis=0)
    return jnp.concatenate([mine, swap_core(mine)], axis=0)


def turn_rows(rows, at):
    zero = jnp.uint32(0)
    grid = rows.reshape(4, 2, 64, rows.shape[1])
    grid = lax.dynamic_slice(jnp.concatenate([grid, grid], axis=0), (at["place"], zero, zero, zero), grid.shape)
    grid = lax.dynamic_slice(jnp.concatenate([grid, grid], axis=1), (zero, at["core"], zero, zero), grid.shape)
    return grid.transpose(1, 0, 2, 3).reshape(rows.shape)


def far_block(rows, index, at):
    return jnp.concatenate(
        [rows_at(rows, at["far"][index], 64), rows_at(rows, at["far_other"][index], 64)], axis=0
    )


def shift_far(parts):
    return [shift_x(parts[0], 2), shift_x(parts[1], 1), shift_x(parts[2], -1)]


def shift_near(line, at):
    sent = line.astype(BF16)
    return [rows_at(line, at["line"][0], 32)] + [
        shift_z(rows_at(sent, at["line"][dz], 32), dz) for dz in (1, 2, 3)
    ]


def take_span(values, span):
    zero = jnp.uint32(0)
    return lax.dynamic_slice(values, (span, zero, zero), (1,) + values.shape[1:])[0]


def body(
    layer_input,
    gate_weight,
    up_weight,
    down_weight,
    out_grad,
    inner_params,
    outer_base,
    outer_momentum,
    span_index,
):
    w_gate = gate_weight[0]
    w_up = up_weight[0]
    w_down = down_weight[0]
    width = w_down.shape[0]
    span = span_index[0].astype(jnp.uint32)
    at = places(lax.axis_index("tpb"))
    at["first"] = at["core"] == 0
    layer_input, out_grad, at, span = together(layer_input, out_grad, at, span)

    inner_span = take_span(inner_params[0], span).astype(F32)
    base_span = take_span(outer_base, span)
    momentum_span = take_span(outer_momentum, span)
    frag_rows, frag_cols = base_span.shape
    pseudo_delta = (base_span - inner_span).reshape(frag_rows, frag_cols // GROUP, GROUP)
    block_scale = (jnp.max(jnp.abs(pseudo_delta), axis=2) + 1e-06).astype(BF16)
    wide_scale = block_scale.astype(F32)[:, :, None]
    code_values = (pseudo_delta / wide_scale).astype(BF16)
    decoded = (code_values.astype(F32) * wide_scale).astype(BF16).reshape(frag_rows, frag_cols)

    blocks_in = gather_far(jnp.concatenate(near_parts(layer_input), axis=0))
    parts_grad = near_parts(out_grad)
    arrived = together(*blocks_in[1:], *parts_grad[1:])
    rows_in = jnp.concatenate(blocks_in[:1] + list(arrived[:3]), axis=0)
    blocks_grad = gather_far(jnp.concatenate(parts_grad[:1] + list(arrived[3:]), axis=0))

    projected = [jnp.dot(rows_in, w, preferred_element_type=F32).astype(BF16) for w in (w_gate, w_up)]
    traded = swap_core(trade_cores(projected, at))
    beside, across = scatter_sends(projected, traded, at)
    beside, across, *blocks_grad = together(shift_sides(beside), shift_y(across, 2), *blocks_grad)
    kept, given = split_cores(beside, at)
    gate_sum, up_sum = scatter_sum(projected, traded, across, kept, swap_core(given), at)
    sigmoid_gate = jax.nn.sigmoid(gate_sum)
    activated = gate_sum * sigmoid_gate
    hidden_part = (activated * up_sum).astype(BF16)
    silu_slope = sigmoid_gate * (1.0 + gate_sum * (1.0 - sigmoid_gate))

    grad_rows = jnp.concatenate(blocks_grad, axis=0)
    back = [lax.dot_general(grad_rows, w_down, TURNED, preferred_element_type=F32).astype(BF16)]
    back_traded = swap_core(trade_cores(back, at))
    back_beside, back_across = scatter_sends(back, back_traded, at)
    hidden_sibling = swap_core(hidden_part)
    hidden_pair = pair_cores(hidden_part, hidden_sibling, at["first"])
    beside = shift_sides(jnp.concatenate([back_beside, hidden_pair], axis=0))
    across = shift_y(jnp.concatenate([back_across, hidden_part], axis=0), 2)

    decoded, hidden_kept = together(decoded, hidden_part)
    other_decoded = lax.ppermute(decoded, "replica", [(0, 1), (1, 0)])
    rows_turned = lax.optimization_barrier(turn_rows(rows_in, at).T)
    grad_ordered = lax.optimization_barrier(turn_rows(grad_rows, at))
    beside, across, other_decoded, rows_turned, grad_ordered = together(
        beside, across, other_decoded, rows_turned, grad_ordered
    )

    kept, given = split_cores(beside[:128], at)
    swapped = swap_core(jnp.concatenate([given, beside[128:], across[64:]], axis=0))
    (hidden_grad,) = scatter_sum(back, back_traded, across[:64], kept, swapped[:64], at)
    hidden_full = paired_rows(
        hidden_kept, hidden_sibling, beside[128:], across[64:], swapped[64:192], swapped[192:], at
    )

    grad_part = jnp.concatenate(
        [(hidden_grad * up_sum * silu_slope).astype(BF16), (hidden_grad * activated).astype(BF16)], axis=1
    )
    grad_blocks = ring_blocks(grad_part)
    out_partial = jnp.dot(hidden_full, w_down, preferred_element_type=F32).astype(BF16)
    *out_parts, out_own = together(*[far_block(out_partial, k, at) for k in (3, 1, 2, 0)])
    out_got = shift_far(out_parts)
    grad_down = lax.dot_general(
        hidden_full, grad_ordered, (((0,), (0,)), ((), ())), preferred_element_type=F32
    ).astype(BF16)[None]
    *arrived, grad_down = together(*grad_blocks[1:], *out_got, grad_down)
    grad_hidden = ring_rows(grad_blocks[:1] + arrived[:3])
    out_got = arrived[3:]
    in_partial = add(
        lax.dot_general(grad_hidden[:, :width], w_gate, TURNED, preferred_element_type=F32),
        lax.dot_general(grad_hidden[:, width:], w_up, TURNED, preferred_element_type=F32),
    ).astype(BF16)
    *in_parts, in_own = together(*[far_block(in_partial, k, at) for k in (3, 1, 2, 0)])
    in_got = shift_far(in_parts)

    grad_hidden, in_own = together(grad_hidden, in_own)
    grad_gate_h, grad_up_h = columns(grad_hidden, 2)
    grad_gate = jnp.dot(rows_turned, grad_gate_h, preferred_element_type=F32).astype(BF16)[None]
    out_line, grad_gate = together(add(*out_got, out_own), grad_gate)
    out_near = shift_near(out_line, at)
    *in_got, out_near[1], out_near[2] = together(*in_got, *out_near[1:3])
    grad_up = jnp.dot(rows_turned, grad_up_h, preferred_element_type=F32).astype(BF16)[None]
    in_near = shift_near(add(*in_got, in_own), at)
    layer_out = add(layer_input, *out_near).astype(BF16)
    grad_input = add(out_grad, *in_near).astype(BF16)

    mean_delta = (decoded.astype(F32) + other_decoded.astype(F32)) / 2
    new_momentum = outer_decay * momentum_span + mean_delta
    new_base = base_span - outer_rate * (mean_delta + outer_decay * new_momentum)
    return (layer_out, grad_input, grad_gate, grad_up, grad_down, new_base, new_momentum)


def solution(mesh):
    return jax.shard_map(
        body,
        mesh=mesh,
        in_specs=(
            P(("replica", "tpa"), "tpb"),
            P("replica", "tpb", "tpa"),
            P("replica", "tpb", "tpa"),
            P("replica", "tpa", "tpb"),
            P(("replica", "tpa"), "tpb"),
            P("replica", None, "tpa", "tpb"),
            P(None, "tpa", "tpb"),
            P(None, "tpa", "tpb"),
            P(),
        ),
        out_specs=(
            P(("replica", "tpa"), "tpb"),
            P(("replica", "tpa"), "tpb"),
            P("replica", "tpb", "tpa"),
            P("replica", "tpb", "tpa"),
            P("replica", "tpa", "tpb"),
            P("tpa", "tpb"),
            P("tpa", "tpb"),
        ),
        check_vma=False,
    )
```

```python
import jax
import jax.numpy as jnp
from jax import lax
from jax.sharding import PartitionSpec as P

GROUP = 128
outer_rate = 0.7
outer_decay = 0.9
F32 = jnp.float32
BF16 = jnp.bfloat16
TURNED = (((1,), (1,)), ((), ()))


def shift_x(values, step):
    return lax.ppermute(values, "tpa", [(i, (i // 4 + step) % 4 * 4 + i % 4) for i in range(16)])


def shift_z(values, step):
    return lax.ppermute(values, "tpa", [(i, i // 4 * 4 + (i + step) % 4) for i in range(16)])


def shift_y(values, step):
    return lax.ppermute(values, "tpb", [(i, (i // 2 + step) % 4 * 2 + i % 2) for i in range(8)])


def swap_core(values):
    return lax.ppermute(values, "tpb", [(i, i ^ 1) for i in range(8)])


def together(*arrays):
    return lax.optimization_barrier(arrays)


def add(*terms):
    total = terms[0].astype(F32)
    for term in terms[1:]:
        total = total + term.astype(F32)
    return total


def near_parts(values):
    return [values] + [shift_z(values, -dz) for dz in (1, 2, 3)]


def gather_far(near):
    return [near, shift_x(near, -1), shift_x(near, 1), shift_x(near, 2)]


def places(index):
    index = index.astype(jnp.uint32)
    core = index & 1
    place = lax.shift_right_logical(index, jnp.uint32(1))
    above = [((place + k) & 3) * 128 for k in range(4)]
    return {
        "place": place,
        "core": core,
        "mine": [start + core * 64 for start in above],
        "theirs": [start + 64 - core * 64 for start in above],
        "far": [((k + 4 - place) & 3) * 64 for k in range(4)],
        "far_other": [((k + 4 - place) & 3) * 64 + 256 for k in range(4)],
        "line": [(core ^ (dz // 2)) * 64 + dz % 2 * 32 for dz in range(4)],
    }


def rows_at(values, start, count):
    return lax.dynamic_slice(values, (start, jnp.uint32(0)), (count, values.shape[1]))


def columns(values, count):
    width = values.shape[1] // count
    return [values[:, k * width : (k + 1) * width] for k in range(count)]


def trade_cores(partials, at):
    return swap_core(
        jnp.concatenate(
            [jnp.concatenate([rows_at(p, start, 64) for start in at["theirs"]], axis=0) for p in partials], axis=1
        )
    )


def chip_sums(partials, got, step, at):
    parts = columns(got[step * 64 : (step + 1) * 64], len(partials))
    return [add(rows_at(p, at["mine"][step], 64), part) for p, part in zip(partials, parts)]


def scatter_sends(partials, got, at):
    return [
        jnp.concatenate([part.astype(BF16) for part in chip_sums(partials, got, step, at)], axis=1)
        for step in (1, 2, 3)
    ]


def scatter_sum(partials, got, arrived, at):
    count = len(partials)
    return [
        add(own, *others)
        for own, *others in zip(chip_sums(partials, got, 0, at), *[columns(part, count) for part in arrived])
    ]


def ring_blocks(own):
    return [own, shift_y(own, -1), shift_y(own, 2), shift_y(own, 1)]


def ring_rows(blocks):
    mine = jnp.concatenate(blocks, axis=0)
    return jnp.concatenate([mine, swap_core(mine)], axis=0)


def turn_rows(rows, at):
    zero = jnp.uint32(0)
    grid = rows.reshape(4, 2, 64, rows.shape[1])
    grid = lax.dynamic_slice(jnp.concatenate([grid, grid], axis=0), (at["place"], zero, zero, zero), grid.shape)
    grid = lax.dynamic_slice(jnp.concatenate([grid, grid], axis=1), (zero, at["core"], zero, zero), grid.shape)
    return grid.transpose(1, 0, 2, 3).reshape(rows.shape)


def far_block(rows, index, at):
    return jnp.concatenate(
        [rows_at(rows, at["far"][index], 64), rows_at(rows, at["far_other"][index], 64)], axis=0
    )


def shift_far(parts):
    return [shift_x(parts[0], 2), shift_x(parts[1], 1), shift_x(parts[2], -1)]


def shift_near(line, at):
    sent = line.astype(BF16)
    return [rows_at(line, at["line"][0], 32)] + [
        shift_z(rows_at(sent, at["line"][dz], 32), dz) for dz in (1, 2, 3)
    ]


def take_span(values, span):
    zero = jnp.uint32(0)
    return lax.dynamic_slice(values, (span, zero, zero), (1,) + values.shape[1:])[0]


def body(
    layer_input,
    gate_weight,
    up_weight,
    down_weight,
    out_grad,
    inner_params,
    outer_base,
    outer_momentum,
    span_index,
):
    w_gate = gate_weight[0]
    w_up = up_weight[0]
    w_down = down_weight[0]
    width = w_down.shape[0]
    span = span_index[0].astype(jnp.uint32)
    at = places(lax.axis_index("tpb"))
    at["first"] = at["core"] == 0
    layer_input, out_grad, at, span = together(layer_input, out_grad, at, span)

    inner_span = take_span(inner_params[0], span).astype(F32)
    base_span = take_span(outer_base, span)
    momentum_span = take_span(outer_momentum, span)
    frag_rows, frag_cols = base_span.shape
    pseudo_delta = (base_span - inner_span).reshape(frag_rows, frag_cols // GROUP, GROUP)
    block_scale = (jnp.max(jnp.abs(pseudo_delta), axis=2) + 1e-06).astype(BF16)
    wide_scale = block_scale.astype(F32)[:, :, None]
    code_values = (pseudo_delta / wide_scale).astype(BF16)
    decoded = (code_values.astype(F32) * wide_scale).astype(BF16).reshape(frag_rows, frag_cols)

    blocks_in = gather_far(jnp.concatenate(near_parts(layer_input), axis=0))
    parts_grad = near_parts(out_grad)
    arrived = together(*blocks_in[1:], *parts_grad[1:])
    rows_in = jnp.concatenate(blocks_in[:1] + list(arrived[:3]), axis=0)
    blocks_grad = gather_far(jnp.concatenate(parts_grad[:1] + list(arrived[3:]), axis=0))

    projected = [jnp.dot(rows_in, w, preferred_element_type=F32).astype(BF16) for w in (w_gate, w_up)]
    traded = trade_cores(projected, at)
    arrived = [shift_y(part, step) for step, part in enumerate(scatter_sends(projected, traded, at), 1)]
    arrived[0], arrived[2], *blocks_grad = together(arrived[0], arrived[2], *blocks_grad)
    gate_sum, up_sum = scatter_sum(projected, traded, arrived, at)
    sigmoid_gate = jax.nn.sigmoid(gate_sum)
    activated = gate_sum * sigmoid_gate
    hidden_part = (activated * up_sum).astype(BF16)
    silu_slope = sigmoid_gate * (1.0 + gate_sum * (1.0 - sigmoid_gate))

    grad_rows = jnp.concatenate(blocks_grad, axis=0)
    back = [lax.dot_general(grad_rows, w_down, TURNED, preferred_element_type=F32).astype(BF16)]
    back_traded = trade_cores(back, at)
    sent = [jnp.concatenate([part, hidden_part], axis=0) for part in scatter_sends(back, back_traded, at)]
    *sent, decoded = together(*sent, decoded)
    arrived = [shift_y(part, step) for step, part in enumerate(sent, 1)]

    other_decoded = lax.ppermute(decoded, "replica", [(0, 1), (1, 0)])
    rows_turned = lax.optimization_barrier(turn_rows(rows_in, at).T)
    grad_ordered = lax.optimization_barrier(turn_rows(grad_rows, at))
    *arrived, other_decoded, rows_turned, grad_ordered = together(
        *arrived, other_decoded, rows_turned, grad_ordered
    )
    (hidden_grad,) = scatter_sum(back, back_traded, [part[:64] for part in arrived], at)
    from_below, from_far, from_above = [part[64:] for part in arrived]
    hidden_full = ring_rows([hidden_part, from_above, from_far, from_below])

    grad_part = jnp.concatenate(
        [(hidden_grad * up_sum * silu_slope).astype(BF16), (hidden_grad * activated).astype(BF16)], axis=1
    )
    grad_blocks = ring_blocks(grad_part)
    out_partial = jnp.dot(hidden_full, w_down, preferred_element_type=F32).astype(BF16)
    *out_parts, out_own = together(*[far_block(out_partial, k, at) for k in (3, 1, 2, 0)])
    out_got = shift_far(out_parts)
    grad_down = lax.dot_general(
        hidden_full, grad_ordered, (((0,), (0,)), ((), ())), preferred_element_type=F32
    ).astype(BF16)[None]
    *arrived, out_got[0], out_got[1], grad_down = together(*grad_blocks[1:], out_got[0], out_got[1], grad_down)
    grad_hidden = ring_rows(grad_blocks[:1] + arrived)
    in_partial = add(
        lax.dot_general(grad_hidden[:, :width], w_gate, TURNED, preferred_element_type=F32),
        lax.dot_general(grad_hidden[:, width:], w_up, TURNED, preferred_element_type=F32),
    ).astype(BF16)
    *in_parts, in_own = together(*[far_block(in_partial, k, at) for k in (3, 1, 2, 0)])
    in_got = shift_far(in_parts)

    grad_hidden, in_own = together(grad_hidden, in_own)
    grad_gate_h, grad_up_h = columns(grad_hidden, 2)
    grad_gate = jnp.dot(rows_turned, grad_gate_h, preferred_element_type=F32).astype(BF16)[None]
    out_line, grad_gate = together(add(*out_got, out_own), grad_gate)
    out_near = shift_near(out_line, at)
    *in_got, out_near[1], out_near[2] = together(*in_got, *out_near[1:3])
    in_near = shift_near(add(*in_got, in_own), at)
    grad_up_h, in_near[1] = together(grad_up_h, in_near[1])
    grad_up = jnp.dot(rows_turned, grad_up_h, preferred_element_type=F32).astype(BF16)[None]
    layer_out = add(layer_input, *out_near).astype(BF16)
    grad_input = add(out_grad, *in_near).astype(BF16)

    mean_delta = (decoded.astype(F32) + other_decoded.astype(F32)) / 2
    new_momentum = outer_decay * momentum_span + mean_delta
    new_base = base_span - outer_rate * (mean_delta + outer_decay * new_momentum)
    return (layer_out, grad_input, grad_gate, grad_up, grad_down, new_base, new_momentum)


def solution(mesh):
    return jax.shard_map(
        body,
        mesh=mesh,
        in_specs=(
            P(("replica", "tpa"), "tpb"),
            P("replica", "tpb", "tpa"),
            P("replica", "tpb", "tpa"),
            P("replica", "tpa", "tpb"),
            P(("replica", "tpa"), "tpb"),
            P("replica", None, "tpa", "tpb"),
            P(None, "tpa", "tpb"),
            P(None, "tpa", "tpb"),
            P(),
        ),
        out_specs=(
            P(("replica", "tpa"), "tpb"),
            P(("replica", "tpa"), "tpb"),
            P("replica", "tpb", "tpa"),
            P("replica", "tpb", "tpa"),
            P("replica", "tpa", "tpb"),
            P("tpa", "tpb"),
            P("tpa", "tpb"),
        ),
        check_vma=False,
    )
```

```python
import jax
import jax.numpy as jnp
from jax import lax
from jax.sharding import PartitionSpec as P

GROUP = 128
outer_rate = 0.7
outer_decay = 0.9
F32 = jnp.float32
BF16 = jnp.bfloat16
TURNED = (((1,), (1,)), ((), ()))


def shift_x(values, step):
    return lax.ppermute(values, "tpa", [(i, (i // 4 + step) % 4 * 4 + i % 4) for i in range(16)])


def shift_z(values, step):
    return lax.ppermute(values, "tpa", [(i, i // 4 * 4 + (i + step) % 4) for i in range(16)])


def shift_y(values, step):
    return lax.ppermute(values, "tpb", [(i, (i // 2 + step) % 4 * 2 + i % 2) for i in range(8)])


def swap_core(values):
    return lax.ppermute(values, "tpb", [(i, i ^ 1) for i in range(8)])


def together(*arrays):
    return lax.optimization_barrier(arrays)


def add(*terms):
    total = terms[0].astype(F32)
    for term in terms[1:]:
        total = total + term.astype(F32)
    return total


def near_parts(values):
    return [values] + [shift_z(values, -dz) for dz in (1, 2, 3)]


def gather_far(near):
    return [near, shift_x(near, -1), shift_x(near, 1), shift_x(near, 2)]


def places(index):
    index = index.astype(jnp.uint32)
    core = index & 1
    place = lax.shift_right_logical(index, jnp.uint32(1))
    above = [((place + k) & 3) * 128 for k in range(4)]
    return {
        "place": place,
        "core": core,
        "mine": [start + core * 64 for start in above],
        "theirs": [start + 64 - core * 64 for start in above],
        "far": [((k + 4 - place) & 3) * 64 for k in range(4)],
        "line": [(core ^ (dz // 2)) * 64 + dz % 2 * 32 for dz in range(4)],
    }


def rows_at(values, start, count):
    return lax.dynamic_slice(values, (start, jnp.uint32(0)), (count, values.shape[1]))


def columns(values, count):
    width = values.shape[1] // count
    return [values[:, k * width : (k + 1) * width] for k in range(count)]


def trade_cores(partials, at):
    return swap_core(
        jnp.concatenate(
            [jnp.concatenate([rows_at(p, start, 64) for start in at["theirs"]], axis=0) for p in partials], axis=1
        )
    )


def chip_sums(partials, got, step, at):
    parts = columns(got[step * 64 : (step + 1) * 64], len(partials))
    return [add(rows_at(p, at["mine"][step], 64), part) for p, part in zip(partials, parts)]


def scatter_sends(partials, got, at):
    return [
        jnp.concatenate([part.astype(BF16) for part in chip_sums(partials, got, step, at)], axis=1)
        for step in (1, 2, 3)
    ]


def scatter_sum(partials, got, arrived, at):
    count = len(partials)
    return [
        add(own, *others)
        for own, *others in zip(chip_sums(partials, got, 0, at), *[columns(part, count) for part in arrived])
    ]


def ring_blocks(own):
    return [own, shift_y(own, -1), shift_y(own, 2), shift_y(own, 1)]


def ring_rows(blocks):
    mine = jnp.concatenate(blocks, axis=0)
    return mine, swap_core(mine)


def turn_rows(rows, at):
    zero = jnp.uint32(0)
    grid = rows.reshape(4, 2, 64, rows.shape[1])
    grid = lax.dynamic_slice(jnp.concatenate([grid, grid], axis=0), (at["place"], zero, zero, zero), grid.shape)
    grid = lax.dynamic_slice(jnp.concatenate([grid, grid], axis=1), (zero, at["core"], zero, zero), grid.shape)
    return grid.transpose(1, 0, 2, 3).reshape(rows.shape)


def far_block(halves, index, at):
    return jnp.concatenate([rows_at(half, at["far"][index], 64) for half in halves], axis=0)


def shift_far(parts):
    return [shift_x(parts[0], 2), shift_x(parts[1], 1), shift_x(parts[2], -1)]


def shift_near(line, at):
    sent = line.astype(BF16)
    return [rows_at(line, at["line"][0], 32)] + [
        shift_z(rows_at(sent, at["line"][dz], 32), dz) for dz in (1, 2, 3)
    ]


def take_span(values, span):
    zero = jnp.uint32(0)
    return lax.dynamic_slice(values, (span, zero, zero), (1,) + values.shape[1:])[0]


def body(
    layer_input,
    gate_weight,
    up_weight,
    down_weight,
    out_grad,
    inner_params,
    outer_base,
    outer_momentum,
    span_index,
):
    w_gate = gate_weight[0]
    w_up = up_weight[0]
    w_down = down_weight[0]
    width = w_down.shape[0]
    span = span_index[0].astype(jnp.uint32)
    at = places(lax.axis_index("tpb"))
    at["first"] = at["core"] == 0
    layer_input, out_grad, at, span = together(layer_input, out_grad, at, span)

    inner_span = take_span(inner_params[0], span).astype(F32)
    base_span = take_span(outer_base, span)
    momentum_span = take_span(outer_momentum, span)
    frag_rows, frag_cols = base_span.shape
    pseudo_delta = (base_span - inner_span).reshape(frag_rows, frag_cols // GROUP, GROUP)
    block_scale = (jnp.max(jnp.abs(pseudo_delta), axis=2) + 1e-06).astype(BF16)
    wide_scale = block_scale.astype(F32)[:, :, None]
    code_values = (pseudo_delta / wide_scale).astype(BF16)
    decoded = (code_values.astype(F32) * wide_scale).astype(BF16).reshape(frag_rows, frag_cols)

    blocks_in = gather_far(jnp.concatenate(near_parts(layer_input), axis=0))
    parts_grad = near_parts(out_grad)
    arrived = together(*blocks_in[1:], *parts_grad[1:])
    rows_in = jnp.concatenate(blocks_in[:1] + list(arrived[:3]), axis=0)
    blocks_grad = gather_far(jnp.concatenate(parts_grad[:1] + list(arrived[3:]), axis=0))

    projected = [jnp.dot(rows_in, w, preferred_element_type=F32).astype(BF16) for w in (w_gate, w_up)]
    traded = trade_cores(projected, at)
    arrived = [shift_y(part, step) for step, part in enumerate(scatter_sends(projected, traded, at), 1)]
    arrived[0], arrived[2], *blocks_grad = together(arrived[0], arrived[2], *blocks_grad)
    gate_sum, up_sum = scatter_sum(projected, traded, arrived, at)
    sigmoid_gate = jax.nn.sigmoid(gate_sum)
    activated = gate_sum * sigmoid_gate
    hidden_part = (activated * up_sum).astype(BF16)
    silu_slope = sigmoid_gate * (1.0 + gate_sum * (1.0 - sigmoid_gate))

    grad_rows = jnp.concatenate(blocks_grad, axis=0)
    back = [lax.dot_general(grad_rows, w_down, TURNED, preferred_element_type=F32).astype(BF16)]
    back_traded = trade_cores(back, at)
    sent = [jnp.concatenate([part, hidden_part], axis=0) for part in scatter_sends(back, back_traded, at)]
    *sent, decoded = together(*sent, decoded)
    arrived = [shift_y(part, step) for step, part in enumerate(sent, 1)]

    other_decoded = lax.ppermute(decoded, "replica", [(0, 1), (1, 0)])
    rows_turned = lax.optimization_barrier(turn_rows(rows_in, at).T)
    grad_ordered = lax.optimization_barrier(turn_rows(grad_rows, at))
    *arrived, other_decoded, rows_turned, grad_ordered = together(
        *arrived, other_decoded, rows_turned, grad_ordered
    )
    (hidden_grad,) = scatter_sum(back, back_traded, [part[:64] for part in arrived], at)
    from_below, from_far, from_above = [part[64:] for part in arrived]
    hidden_halves = ring_rows([hidden_part, from_above, from_far, from_below])

    grad_part = jnp.concatenate(
        [(hidden_grad * up_sum * silu_slope).astype(BF16), (hidden_grad * activated).astype(BF16)], axis=1
    )
    grad_blocks = ring_blocks(grad_part)
    hidden_full = jnp.concatenate(hidden_halves, axis=0)
    out_partial = [jnp.dot(half, w_down, preferred_element_type=F32).astype(BF16) for half in hidden_halves]
    *out_parts, out_own = together(*[far_block(out_partial, k, at) for k in (3, 1, 2, 0)])
    out_got = shift_far(out_parts)
    grad_down = lax.dot_general(
        hidden_full, grad_ordered, (((0,), (0,)), ((), ())), preferred_element_type=F32
    ).astype(BF16)[None]
    *arrived, out_got[0], grad_down = together(*grad_blocks[1:], out_got[0], grad_down)
    grad_halves = ring_rows(grad_blocks[:1] + arrived)
    grad_hidden = jnp.concatenate(grad_halves, axis=0)
    in_partial = [
        add(
            lax.dot_general(half[:, :width], w_gate, TURNED, preferred_element_type=F32),
            lax.dot_general(half[:, width:], w_up, TURNED, preferred_element_type=F32),
        ).astype(BF16)
        for half in grad_halves
    ]
    *in_parts, in_own = together(*[far_block(in_partial, k, at) for k in (3, 1, 2, 0)])
    in_got = shift_far(in_parts)

    grad_hidden, in_own = together(grad_hidden, in_own)
    grad_gate_h, grad_up_h = columns(grad_hidden, 2)
    out_got[1], out_got[2], in_own = together(out_got[1], out_got[2], in_own)
    grad_gate = jnp.dot(rows_turned, grad_gate_h, preferred_element_type=F32).astype(BF16)[None]
    out_line, grad_gate = together(add(*out_got, out_own), grad_gate)
    out_near = shift_near(out_line, at)
    *in_got, out_near[1], out_near[2] = together(*in_got, *out_near[1:3])
    in_near = shift_near(add(*in_got, in_own), at)
    grad_up_h, in_near[1] = together(grad_up_h, in_near[1])
    grad_up = jnp.dot(rows_turned, grad_up_h, preferred_element_type=F32).astype(BF16)[None]
    layer_out = add(layer_input, *out_near).astype(BF16)
    grad_input = add(out_grad, *in_near).astype(BF16)

    mean_delta = (decoded.astype(F32) + other_decoded.astype(F32)) / 2
    new_momentum = outer_decay * momentum_span + mean_delta
    new_base = base_span - outer_rate * (mean_delta + outer_decay * new_momentum)
    return (layer_out, grad_input, grad_gate, grad_up, grad_down, new_base, new_momentum)


def solution(mesh):
    return jax.shard_map(
        body,
        mesh=mesh,
        in_specs=(
            P(("replica", "tpa"), "tpb"),
            P("replica", "tpb", "tpa"),
            P("replica", "tpb", "tpa"),
            P("replica", "tpa", "tpb"),
            P(("replica", "tpa"), "tpb"),
            P("replica", None, "tpa", "tpb"),
            P(None, "tpa", "tpb"),
            P(None, "tpa", "tpb"),
            P(),
        ),
        out_specs=(
            P(("replica", "tpa"), "tpb"),
            P(("replica", "tpa"), "tpb"),
            P("replica", "tpb", "tpa"),
            P("replica", "tpb", "tpa"),
            P("replica", "tpa", "tpb"),
            P("tpa", "tpb"),
            P("tpa", "tpb"),
        ),
        check_vma=False,
    )
```

```python
import jax
import jax.numpy as jnp
from jax import lax
from jax.sharding import PartitionSpec as P

GROUP = 128
outer_rate = 0.7
outer_decay = 0.9
F32 = jnp.float32
BF16 = jnp.bfloat16
TURNED = (((1,), (1,)), ((), ()))


def shift_x(values, step):
    return lax.ppermute(values, "tpa", [(i, (i // 4 ^ step) * 4 + i % 4) for i in range(16)])


def shift_z(values, step):
    return lax.ppermute(values, "tpa", [(i, i // 4 * 4 + (i % 4 ^ step)) for i in range(16)])


def shift_y(values, step):
    return lax.ppermute(values, "tpb", [(i, (i // 2 ^ step) * 2 + i % 2) for i in range(8)])


def swap_core(values):
    return lax.ppermute(values, "tpb", [(i, i ^ 1) for i in range(8)])


def together(*arrays):
    return lax.optimization_barrier(arrays)


def add(*terms):
    total = terms[0].astype(F32)
    for term in terms[1:]:
        total = total + term.astype(F32)
    return total


def near_parts(values):
    return [values] + [shift_z(values, dz) for dz in (1, 2, 3)]


def gather_far(near):
    return [near, shift_x(near, 1), shift_x(near, 3), shift_x(near, 2)]


def places(index):
    index = index.astype(jnp.uint32)
    core = index & 1
    place = lax.shift_right_logical(index, jnp.uint32(1))
    above = [(place ^ k) * 128 for k in range(4)]
    return {
        "bits": [lax.shift_right_logical(place, jnp.uint32(1)), place & 1, core],
        "core": core,
        "mine": [start + core * 64 for start in above],
        "theirs": [start + 64 - core * 64 for start in above],
        "far": [(place ^ k) * 64 for k in range(4)],
        "line": [(core ^ (dz // 2)) * 64 + dz % 2 * 32 for dz in range(4)],
    }


def rows_at(values, start, count):
    return lax.dynamic_slice(values, (start, jnp.uint32(0)), (count, values.shape[1]))


def columns(values, count):
    width = values.shape[1] // count
    return [values[:, k * width : (k + 1) * width] for k in range(count)]


def trade_cores(partials, at):
    return swap_core(
        jnp.concatenate(
            [jnp.concatenate([rows_at(p, start, 64) for start in at["theirs"]], axis=0) for p in partials], axis=1
        )
    )


def chip_sums(partials, got, step, at):
    parts = columns(got[step * 64 : (step + 1) * 64], len(partials))
    return [add(rows_at(p, at["mine"][step], 64), part) for p, part in zip(partials, parts)]


def scatter_sends(partials, got, at):
    return [
        jnp.concatenate([part.astype(BF16) for part in chip_sums(partials, got, step, at)], axis=1)
        for step in (1, 2, 3)
    ]


def scatter_sum(partials, got, arrived, at):
    count = len(partials)
    return [
        add(own, *others)
        for own, *others in zip(chip_sums(partials, got, 0, at), *[columns(part, count) for part in arrived])
    ]


def ring_blocks(own):
    return [own, shift_y(own, 1), shift_y(own, 2), shift_y(own, 3)]


def ring_rows(blocks):
    mine = jnp.concatenate(blocks, axis=0)
    return mine, swap_core(mine)


def turn_rows(rows, at):
    zero = jnp.uint32(0)
    grid = rows.reshape(2, 2, 2, 64, rows.shape[1])
    for axis, bit in enumerate(at["bits"]):
        start = [zero] * 5
        start[axis] = bit
        grid = lax.dynamic_slice(jnp.concatenate([grid, grid], axis=axis), start, grid.shape)
    return grid.transpose(2, 0, 1, 3, 4).reshape(rows.shape)


def far_block(halves, index, at):
    return jnp.concatenate([rows_at(half, at["far"][index], 64) for half in halves], axis=0)


def shift_far(parts):
    return [shift_x(parts[0], 2), shift_x(parts[1], 1), shift_x(parts[2], 3)]


def shift_near(line, at):
    sent = line.astype(BF16)
    return [rows_at(line, at["line"][0], 32)] + [
        shift_z(rows_at(sent, at["line"][dz], 32), dz) for dz in (1, 2, 3)
    ]


def take_span(values, span):
    zero = jnp.uint32(0)
    return lax.dynamic_slice(values, (span, zero, zero), (1,) + values.shape[1:])[0]


def body(
    layer_input,
    gate_weight,
    up_weight,
    down_weight,
    out_grad,
    inner_params,
    outer_base,
    outer_momentum,
    span_index,
):
    w_gate = gate_weight[0]
    w_up = up_weight[0]
    w_down = down_weight[0]
    width = w_down.shape[0]
    span = span_index[0].astype(jnp.uint32)
    at = places(lax.axis_index("tpb"))
    at["first"] = at["core"] == 0
    layer_input, out_grad, at, span = together(layer_input, out_grad, at, span)

    inner_span = take_span(inner_params[0], span).astype(F32)
    base_span = take_span(outer_base, span)
    momentum_span = take_span(outer_momentum, span)
    frag_rows, frag_cols = base_span.shape
    pseudo_delta = (base_span - inner_span).reshape(frag_rows, frag_cols // GROUP, GROUP)
    block_scale = (jnp.max(jnp.abs(pseudo_delta), axis=2) + 1e-06).astype(BF16)
    wide_scale = block_scale.astype(F32)[:, :, None]
    code_values = (pseudo_delta / wide_scale).astype(BF16)
    decoded = (code_values.astype(F32) * wide_scale).astype(BF16).reshape(frag_rows, frag_cols)

    blocks_in = gather_far(jnp.concatenate(near_parts(layer_input), axis=0))
    parts_grad = near_parts(out_grad)
    arrived = together(*blocks_in[1:], *parts_grad[1:])
    rows_in = jnp.concatenate(blocks_in[:1] + list(arrived[:3]), axis=0)
    blocks_grad = gather_far(jnp.concatenate(parts_grad[:1] + list(arrived[3:]), axis=0))

    projected = [jnp.dot(rows_in, w, preferred_element_type=F32).astype(BF16) for w in (w_gate, w_up)]
    traded = trade_cores(projected, at)
    arrived = [shift_y(part, step) for step, part in enumerate(scatter_sends(projected, traded, at), 1)]
    arrived[0], arrived[2], *blocks_grad = together(arrived[0], arrived[2], *blocks_grad)
    gate_sum, up_sum = scatter_sum(projected, traded, arrived, at)
    sigmoid_gate = jax.nn.sigmoid(gate_sum)
    activated = gate_sum * sigmoid_gate
    hidden_part = (activated * up_sum).astype(BF16)
    silu_slope = sigmoid_gate * (1.0 + gate_sum * (1.0 - sigmoid_gate))

    grad_rows = jnp.concatenate(blocks_grad, axis=0)
    back = [lax.dot_general(grad_rows, w_down, TURNED, preferred_element_type=F32).astype(BF16)]
    back_traded = trade_cores(back, at)
    sent = [jnp.concatenate([part, hidden_part], axis=0) for part in scatter_sends(back, back_traded, at)]
    *sent, decoded = together(*sent, decoded)
    arrived = [shift_y(part, step) for step, part in enumerate(sent, 1)]

    other_decoded = lax.ppermute(decoded, "replica", [(0, 1), (1, 0)])
    rows_turned = lax.optimization_barrier(turn_rows(rows_in, at).T)
    grad_ordered = lax.optimization_barrier(turn_rows(grad_rows, at))
    *arrived, other_decoded, rows_turned, grad_ordered = together(
        *arrived, other_decoded, rows_turned, grad_ordered
    )
    (hidden_grad,) = scatter_sum(back, back_traded, [part[:64] for part in arrived], at)
    hidden_halves = ring_rows([hidden_part] + [part[64:] for part in arrived])

    grad_part = jnp.concatenate(
        [(hidden_grad * up_sum * silu_slope).astype(BF16), (hidden_grad * activated).astype(BF16)], axis=1
    )
    grad_blocks = ring_blocks(grad_part)
    hidden_full = jnp.concatenate(hidden_halves, axis=0)
    out_partial = [jnp.dot(half, w_down, preferred_element_type=F32).astype(BF16) for half in hidden_halves]
    *out_parts, out_own = together(*[far_block(out_partial, k, at) for k in (3, 1, 2, 0)])
    out_got = shift_far(out_parts)
    grad_down = lax.dot_general(
        hidden_full, grad_ordered, (((0,), (0,)), ((), ())), preferred_element_type=F32
    ).astype(BF16)[None]
    *arrived, out_got[0], grad_down = together(*grad_blocks[1:], out_got[0], grad_down)
    grad_halves = ring_rows(grad_blocks[:1] + arrived)
    grad_hidden = jnp.concatenate(grad_halves, axis=0)
    in_partial = [
        add(
            lax.dot_general(half[:, :width], w_gate, TURNED, preferred_element_type=F32),
            lax.dot_general(half[:, width:], w_up, TURNED, preferred_element_type=F32),
        ).astype(BF16)
        for half in grad_halves
    ]
    *in_parts, in_own = together(*[far_block(in_partial, k, at) for k in (3, 1, 2, 0)])
    in_got = shift_far(in_parts)

    grad_hidden, in_own = together(grad_hidden, in_own)
    grad_gate_h, grad_up_h = columns(grad_hidden, 2)
    out_got[1], out_got[2], in_own = together(out_got[1], out_got[2], in_own)
    grad_gate = jnp.dot(rows_turned, grad_gate_h, preferred_element_type=F32).astype(BF16)[None]
    out_line, grad_gate = together(add(*out_got, out_own), grad_gate)
    out_near = shift_near(out_line, at)
    *in_got, out_near[1], out_near[2] = together(*in_got, *out_near[1:3])
    in_near = shift_near(add(*in_got, in_own), at)
    grad_up_h, in_near[1] = together(grad_up_h, in_near[1])
    grad_up = jnp.dot(rows_turned, grad_up_h, preferred_element_type=F32).astype(BF16)[None]
    layer_out = add(layer_input, *out_near).astype(BF16)
    grad_input = add(out_grad, *in_near).astype(BF16)

    mean_delta = (decoded.astype(F32) + other_decoded.astype(F32)) / 2
    new_momentum = outer_decay * momentum_span + mean_delta
    new_base = base_span - outer_rate * (mean_delta + outer_decay * new_momentum)
    return (layer_out, grad_input, grad_gate, grad_up, grad_down, new_base, new_momentum)


def solution(mesh):
    return jax.shard_map(
        body,
        mesh=mesh,
        in_specs=(
            P(("replica", "tpa"), "tpb"),
            P("replica", "tpb", "tpa"),
            P("replica", "tpb", "tpa"),
            P("replica", "tpa", "tpb"),
            P(("replica", "tpa"), "tpb"),
            P("replica", None, "tpa", "tpb"),
            P(None, "tpa", "tpb"),
            P(None, "tpa", "tpb"),
            P(),
        ),
        out_specs=(
            P(("replica", "tpa"), "tpb"),
            P(("replica", "tpa"), "tpb"),
            P("replica", "tpb", "tpa"),
            P("replica", "tpb", "tpa"),
            P("replica", "tpa", "tpb"),
            P("tpa", "tpb"),
            P("tpa", "tpb"),
        ),
        check_vma=False,
    )
```

```python
import jax
import jax.numpy as jnp
from jax import lax
from jax.sharding import PartitionSpec as P

GROUP = 128
outer_rate = 0.7
outer_decay = 0.9
F32 = jnp.float32
BF16 = jnp.bfloat16
TURNED = (((1,), (1,)), ((), ()))


def shift_x(values, step):
    return lax.ppermute(values, "tpa", [(i, (i // 4 + step) % 4 * 4 + i % 4) for i in range(16)])


def shift_z(values, step):
    return lax.ppermute(values, "tpa", [(i, i // 4 * 4 + (i + step) % 4) for i in range(16)])


def shift_y(values, step):
    return lax.ppermute(values, "tpb", [(i, (i // 2 + step) % 4 * 2 + i % 2) for i in range(8)])


def swap_core(values):
    return lax.ppermute(values, "tpb", [(i, i ^ 1) for i in range(8)])


def together(*arrays):
    return lax.optimization_barrier(arrays)


def add(*terms):
    total = terms[0].astype(F32)
    for term in terms[1:]:
        total = total + term.astype(F32)
    return total


def near_parts(values):
    return [values] + [shift_z(values, -dz) for dz in (1, 2, 3)]


def gather_far(near):
    return [near, shift_x(near, -1), shift_x(near, 1), shift_x(near, 2)]


def places(index):
    index = index.astype(jnp.uint32)
    core = index & 1
    place = lax.shift_right_logical(index, jnp.uint32(1))
    above = [((place + k) & 3) * 128 for k in range(4)]
    return {
        "place": place,
        "core": core,
        "mine": [start + core * 64 for start in above],
        "theirs": [start + 64 - core * 64 for start in above],
        "far": [((k + 4 - place) & 3) * 64 for k in range(4)],
        "line": [(core ^ (dz // 2)) * 64 + dz % 2 * 32 for dz in range(4)],
    }


def rows_at(values, start, count):
    return lax.dynamic_slice(values, (start, jnp.uint32(0)), (count, values.shape[1]))


def columns(values, count):
    width = values.shape[1] // count
    return [values[:, k * width : (k + 1) * width] for k in range(count)]


def trade_cores(partials, at):
    return swap_core(
        jnp.concatenate(
            [jnp.concatenate([rows_at(p, start, 64) for start in at["theirs"]], axis=0) for p in partials], axis=1
        )
    )


def chip_sums(partials, got, step, at):
    parts = columns(got[step * 64 : (step + 1) * 64], len(partials))
    return [add(rows_at(p, at["mine"][step], 64), part) for p, part in zip(partials, parts)]


def scatter_sends(partials, got, at):
    return [
        jnp.concatenate([part.astype(BF16) for part in chip_sums(partials, got, step, at)], axis=1)
        for step in (1, 2, 3)
    ]


def scatter_sum(partials, got, arrived, at):
    count = len(partials)
    return [
        add(own, *others)
        for own, *others in zip(chip_sums(partials, got, 0, at), *[columns(part, count) for part in arrived])
    ]


def ring_blocks(own):
    return [own, shift_y(own, -1), shift_y(own, 2), shift_y(own, 1)]


def ring_rows(blocks):
    mine = jnp.concatenate(blocks, axis=0)
    return mine, swap_core(mine)


def turn_rows(rows, at):
    zero = jnp.uint32(0)
    grid = rows.reshape(4, 2, 64, rows.shape[1])
    grid = lax.dynamic_slice(jnp.concatenate([grid, grid], axis=0), (at["place"], zero, zero, zero), grid.shape)
    grid = lax.dynamic_slice(jnp.concatenate([grid, grid], axis=1), (zero, at["core"], zero, zero), grid.shape)
    return grid.transpose(1, 0, 2, 3).reshape(rows.shape)


def far_block(halves, index, at):
    return jnp.concatenate([rows_at(half, at["far"][index], 64) for half in halves], axis=0)


def shift_far(parts):
    return [shift_x(parts[0], 2), shift_x(parts[1], 1), shift_x(parts[2], -1)]


def shift_near(line, at):
    sent = line.astype(BF16)
    return [rows_at(line, at["line"][0], 32)] + [
        shift_z(rows_at(sent, at["line"][dz], 32), dz) for dz in (1, 2, 3)
    ]


def take_span(values, span):
    zero = jnp.uint32(0)
    return lax.dynamic_slice(values, (span, zero, zero), (1,) + values.shape[1:])[0]


def body(
    layer_input,
    gate_weight,
    up_weight,
    down_weight,
    out_grad,
    inner_params,
    outer_base,
    outer_momentum,
    span_index,
):
    w_gate = gate_weight[0]
    w_up = up_weight[0]
    w_down = down_weight[0]
    width = w_down.shape[0]
    span = span_index[0].astype(jnp.uint32)
    at = places(lax.axis_index("tpb"))
    at["first"] = at["core"] == 0
    layer_input, out_grad, at, span = together(layer_input, out_grad, at, span)

    inner_span = take_span(inner_params[0], span).astype(F32)
    base_span = take_span(outer_base, span)
    momentum_span = take_span(outer_momentum, span)
    frag_rows, frag_cols = base_span.shape
    pseudo_delta = (base_span - inner_span).reshape(frag_rows, frag_cols // GROUP, GROUP)
    block_scale = (jnp.max(jnp.abs(pseudo_delta), axis=2) + 1e-06).astype(BF16)
    wide_scale = block_scale.astype(F32)[:, :, None]
    code_values = (pseudo_delta / wide_scale).astype(BF16)
    decoded = (code_values.astype(F32) * wide_scale).astype(BF16).reshape(frag_rows, frag_cols)

    parts_in = near_parts(layer_input)
    parts_grad = near_parts(out_grad)
    *parts_in, parts_grad[1] = together(*parts_in, parts_grad[1])
    blocks_in = gather_far(jnp.concatenate(parts_in, axis=0))
    arrived = together(*blocks_in[1:], *parts_grad[1:])
    rows_in = jnp.concatenate(blocks_in[:1] + list(arrived[:3]), axis=0)
    blocks_grad = gather_far(jnp.concatenate(parts_grad[:1] + list(arrived[3:]), axis=0))

    projected = [jnp.dot(rows_in, w, preferred_element_type=F32).astype(BF16) for w in (w_gate, w_up)]
    traded = trade_cores(projected, at)
    arrived = [shift_y(part, step) for step, part in enumerate(scatter_sends(projected, traded, at), 1)]
    arrived[0], arrived[2], *blocks_grad = together(arrived[0], arrived[2], *blocks_grad)
    gate_sum, up_sum = scatter_sum(projected, traded, arrived, at)
    sigmoid_gate = jax.nn.sigmoid(gate_sum)
    activated = gate_sum * sigmoid_gate
    hidden_part = (activated * up_sum).astype(BF16)
    silu_slope = sigmoid_gate * (1.0 + gate_sum * (1.0 - sigmoid_gate))

    grad_rows = jnp.concatenate(blocks_grad, axis=0)
    back = [lax.dot_general(grad_rows, w_down, TURNED, preferred_element_type=F32).astype(BF16)]
    back_traded = trade_cores(back, at)
    sent = [jnp.concatenate([part, hidden_part], axis=0) for part in scatter_sends(back, back_traded, at)]
    *sent, decoded = together(*sent, decoded)
    arrived = [shift_y(part, step) for step, part in enumerate(sent, 1)]

    other_decoded = lax.ppermute(decoded, "replica", [(0, 1), (1, 0)])
    rows_turned = lax.optimization_barrier(turn_rows(rows_in, at).T)
    grad_ordered = lax.optimization_barrier(turn_rows(grad_rows, at))
    *arrived, other_decoded, rows_turned, grad_ordered = together(
        *arrived, other_decoded, rows_turned, grad_ordered
    )
    (hidden_grad,) = scatter_sum(back, back_traded, [part[:64] for part in arrived], at)
    from_below, from_far, from_above = [part[64:] for part in arrived]
    hidden_halves = ring_rows([hidden_part, from_above, from_far, from_below])

    grad_part = jnp.concatenate(
        [(hidden_grad * up_sum * silu_slope).astype(BF16), (hidden_grad * activated).astype(BF16)], axis=1
    )
    grad_blocks = ring_blocks(grad_part)
    hidden_full = jnp.concatenate(hidden_halves, axis=0)
    out_partial = [jnp.dot(half, w_down, preferred_element_type=F32).astype(BF16) for half in hidden_halves]
    *out_parts, out_own = together(*[far_block(out_partial, k, at) for k in (3, 1, 2, 0)])
    out_got = shift_far(out_parts)
    grad_down = lax.dot_general(
        hidden_full, grad_ordered, (((0,), (0,)), ((), ())), preferred_element_type=F32
    ).astype(BF16)[None]
    *arrived, out_got[0], grad_down = together(*grad_blocks[1:], out_got[0], grad_down)
    grad_halves = ring_rows(grad_blocks[:1] + arrived)
    grad_hidden = jnp.concatenate(grad_halves, axis=0)
    in_partial = [
        add(
            lax.dot_general(half[:, :width], w_gate, TURNED, preferred_element_type=F32),
            lax.dot_general(half[:, width:], w_up, TURNED, preferred_element_type=F32),
        ).astype(BF16)
        for half in grad_halves
    ]
    *in_parts, in_own = together(*[far_block(in_partial, k, at) for k in (3, 1, 2, 0)])
    in_got = shift_far(in_parts)

    grad_hidden, in_own = together(grad_hidden, in_own)
    grad_gate_h, grad_up_h = columns(grad_hidden, 2)
    out_got[1], out_got[2], in_own = together(out_got[1], out_got[2], in_own)
    grad_gate = jnp.dot(rows_turned, grad_gate_h, preferred_element_type=F32).astype(BF16)[None]
    out_line, grad_gate = together(add(*out_got, out_own), grad_gate)
    out_near = shift_near(out_line, at)
    *in_got, out_near[1], out_near[2] = together(*in_got, *out_near[1:3])
    in_near = shift_near(add(*in_got, in_own), at)
    grad_up_h, in_near[1] = together(grad_up_h, in_near[1])
    grad_up = jnp.dot(rows_turned, grad_up_h, preferred_element_type=F32).astype(BF16)[None]
    layer_out = add(layer_input, *out_near).astype(BF16)
    grad_input = add(out_grad, *in_near).astype(BF16)

    mean_delta = (decoded.astype(F32) + other_decoded.astype(F32)) / 2
    new_momentum = outer_decay * momentum_span + mean_delta
    new_base = base_span - outer_rate * (mean_delta + outer_decay * new_momentum)
    return (layer_out, grad_input, grad_gate, grad_up, grad_down, new_base, new_momentum)


def solution(mesh):
    return jax.shard_map(
        body,
        mesh=mesh,
        in_specs=(
            P(("replica", "tpa"), "tpb"),
            P("replica", "tpb", "tpa"),
            P("replica", "tpb", "tpa"),
            P("replica", "tpa", "tpb"),
            P(("replica", "tpa"), "tpb"),
            P("replica", None, "tpa", "tpb"),
            P(None, "tpa", "tpb"),
            P(None, "tpa", "tpb"),
            P(),
        ),
        out_specs=(
            P(("replica", "tpa"), "tpb"),
            P(("replica", "tpa"), "tpb"),
            P("replica", "tpb", "tpa"),
            P("replica", "tpb", "tpa"),
            P("replica", "tpa", "tpb"),
            P("tpa", "tpb"),
            P("tpa", "tpb"),
        ),
        check_vma=False,
    )
```
